32 devices in a mesh: shot: 4 (over z), space: 8 (over y, x, core).
Axes of the slice: x: 2, y: 2, z: 4, core: 2. Of those that a mesh axis runs over, the one named last changes fastest.
Arguments:
- courant: float32 [32, 256, 128], P('space'), may hold values from 0.02 to 0.18
- adjoint_now: float32 [4, 32, 256, 128], P('shot', 'space'), may hold values from -6 to 6
- adjoint_old: float32 [4, 32, 256, 128], P('shot', 'space'), may hold values from -6 to 6
- receiver_slab: int32 [4, 3072, 1], P('shot', 'space'), may hold values from 0 to 7; in each aligned block of 384 rows (0 to 383, 384 to 767, ..., all dimensions but the last counted through in order) at most 48 rows name the same one
- receiver_cell: int32 [4, 3072], P('shot', 'space'), may hold values from 0 to 131071
- residuals: float32 [4, 3, 3072], P('shot', None, 'space'), may hold values from -24 to 24
- forward_field: bfloat16 [4, 3, 32, 256, 128], P('shot', None, 'space'), may hold values from -6 to 6
Outputs:
- adjoint_last: float32 [4, 32, 256, 128], P('shot', 'space')
- adjoint_prior: float32 [4, 32, 256, 128], P('shot', 'space')
- gradient_image: float32 [32, 256, 128], P('space', 'shot')
The draws below stay inside these ranges and needn't reach their ends.
Inputs may be any that keep to these rules, and one draw needn't show every extreme that they name: `receiver_slab`: in each aligned block of 384 receivers (those held by one index of space) at most 48 lie in one slab, and some block reaches 48.
All inputs are finite; a program needn't handle non-finite values.
Results may differ from the reference program's by a relative error of at most 0.0003.
Values sent between devices are 32-bit elements; how exact they have to be, the bound alone decides.
A program may use at most 64 MiB of HBM per device.

```python
import math
import jax
import jax.numpy as jnp
import numpy as np
from jax import lax

CX = 4
NY = 256
NZ = 128
STEPS = 3
REC_DEV = 384
CAP = 48
NX = 32
REC = 3072
SHOTS = 4
N_SPACE = 8


def place_ends(drawn, stream_key, smallest, largest):
    longest = drawn.shape.index(max(drawn.shape))
    spots = []
    for shift in (0, 1):
        where = [jax.random.randint(jax.random.fold_in(stream_key, axis), (), 0, length) for axis, length in enumerate(drawn.shape)]
        where[longest] = (where[longest] + shift) % drawn.shape[longest]
        spots.append(tuple(where))
    return drawn.at[spots[0]].set(smallest).at[spots[1]].set(largest)


def spiked(values, rng, source, target, shards_of, factor):
    def block_of(axis_at):
        return (jnp.arange(values.shape[axis_at]) // (values.shape[axis_at] // shards_of)).reshape((-1,) + (1,) * (values.ndim - 1 - axis_at))

    one_side = jax.random.permutation(rng, shards_of)[block_of(target)]
    second = (block_of(target) + shards_of // 2) % shards_of
    return jnp.where((block_of(source) == one_side) | (block_of(source) == second), factor * values, values)


def levels(key, shape, cuts, smallest, largest):
    def one(dim, shards_of):
        heights = jax.random.uniform(jax.random.fold_in(jax.random.fold_in(key, 6), dim), (shards_of,), jnp.float32, smallest / len(cuts), largest / len(cuts))
        return jnp.repeat(jnp.exp(heights), shape[dim] // shards_of).reshape((-1,) + (1,) * (len(shape) - dim - 1))

    level = one(*cuts[0])
    for cut in cuts[1:]:
        level = level * one(*cut)
    return level


def routed_block(key, own, number, rows, amount, top, most, lean):
    order = jax.random.permutation(key, amount)
    heavy_load, usual = shares(amount, rows * top, most, lean, True), shares(amount, rows * top, most, lean, False)
    places = jnp.arange(amount)

    def named(sizes, rotation):
        used = int((sizes > 0).sum())
        fixed = max(1, used // 4)
        passed = fixed + (places - fixed + rotation * (used - fixed)) % max(1, amount - fixed)
        return jnp.zeros((amount,), jnp.int32).at[order[jnp.where(places < fixed, places, passed)]].set(jnp.asarray(sizes, jnp.int32))

    sizes = jnp.where(number % 4 == 0, named(heavy_load, number // 4), named(usual, number - number // 4 - 1))
    mixed = jax.random.permutation(jax.random.fold_in(own, 3), amount)
    source_of, receiver = mixed[0:amount // 2 * 2:2], mixed[1:amount // 2 * 2:2]
    margin = jnp.minimum(sizes[source_of] - 1, most - sizes[receiver]) // 2
    margin = jnp.where((source_of == order[0]) | (receiver == order[0]) | (sizes[receiver] == 0), 0, jnp.maximum(margin, 0))
    passed = jax.random.randint(jax.random.fold_in(own, 4), (amount // 2,), 0, 1 << 20) % (margin + 1)
    sizes = sizes.at[source_of].add(-passed).at[receiver].add(passed)
    members = jnp.searchsorted(jnp.cumsum(sizes), jnp.arange(rows * top), side="right").astype(jnp.int32)
    listing = members.reshape(top, rows).T
    listing = listing[jax.random.permutation(jax.random.fold_in(own, 1), rows)]
    rotation = jax.random.randint(jax.random.fold_in(own, 2), (rows, 1), 0, top)
    return jnp.take_along_axis(listing, (jnp.arange(top)[None, :] + rotation) % top, axis=1)


def shares(amount, total, limit, lean, full):
    portions = [(1 << 20) // math.isqrt(standing ** lean) + 1 for standing in range(1, amount + 1)]
    largest = limit if full else min(limit, max(-(-total // amount), total * portions[0] // sum(portions)))
    least = 1 if total - largest >= amount - 1 else 0
    counts, spare = [largest] + [least] * (amount - 1), total - largest - least * (amount - 1)
    while spare > 0:
        movable = [i for i in range(1, amount) if counts[i] < largest] or [i for i in range(1, amount) if counts[i] < limit]
        mass, budget = sum([portions[i] for i in movable]), spare
        for i in movable:
            more = min(limit - counts[i], max(1, budget * portions[i] // mass), spare)
            counts[i] = counts[i] + more
            spare = spare - more
    return np.array(counts)


def bell_draw(rng, shape, spread, bound, shards=(), dtype=jnp.bfloat16):
    array = spread * jax.random.normal(rng, shape, jnp.float32)
    if shards:
        array = array * levels(rng, shape, shards, -0.22, 0.18)
    return jnp.clip(array, -bound, bound).astype(dtype)


def bell_draw_with(rng, extent, width, most, shards, heavy, held_as=jnp.bfloat16):
    drawn = width * jax.random.normal(rng, extent, jnp.float32)
    if shards:
        drawn = drawn * levels(rng, extent, shards, -0.22, 0.18)
    return jnp.clip(spiked(drawn, jax.random.fold_in(rng, 3), *heavy), -most, most).astype(held_as)


def setup_inputs(seed: int = 0) -> dict:
    arg_keys = jax.random.split(jax.random.key(seed), 8)
    courant = jnp.clip(jnp.exp(math.log(0.18) - 2.1972246 * jax.random.uniform(arg_keys[0], (NX, NY, NZ), jnp.float32) ** levels(arg_keys[0], (NX, NY, NZ), ((0, 8),), -0.2, 0.2)), 0.02, 0.18)
    adjoint_now = bell_draw(arg_keys[1], (SHOTS, NX, NY, NZ), 1.0, 6.0, ((0, 4), (1, 8)), jnp.float32)
    adjoint_old = bell_draw(arg_keys[2], (SHOTS, NX, NY, NZ), 1.0, 6.0, ((0, 4), (1, 8)), jnp.float32)
    receiver_slab_keys = jax.random.split(jax.random.fold_in(arg_keys[3], 1), SHOTS * REC // REC_DEV)
    receiver_slab_turns = jax.random.permutation(jax.random.fold_in(arg_keys[3], 3), SHOTS * REC // REC_DEV)
    receiver_slab = jax.vmap(lambda own, number: routed_block(jax.random.fold_in(arg_keys[3], 2), own, number, REC_DEV, N_SPACE, 1, CAP, 2))(receiver_slab_keys, receiver_slab_turns).reshape((SHOTS, REC, 1))
    receiver_cell = place_ends(jax.random.randint(arg_keys[4], (SHOTS, REC), 0, CX * NY * NZ), jax.random.fold_in(arg_keys[4], 1), 0, (CX * NY * NZ) - 1).astype(jnp.int32)
    residuals = bell_draw(arg_keys[5], (SHOTS, STEPS, REC), 4.0, 24.0, ((0, 4), (2, 8)), jnp.float32)
    forward_field = bell_draw_with(arg_keys[6], (SHOTS, STEPS, NX, NY, NZ), 1.0, 6.0, ((0, 4), (2, 8)), (0, 3, 4, 2.0))
    return {"courant": courant, "adjoint_now": adjoint_now, "adjoint_old": adjoint_old, "receiver_slab": receiver_slab, "receiver_cell": receiver_cell, "residuals": residuals, "forward_field": forward_field}


STENCIL_WEIGHTS = (-205.0 / 72.0, 8.0 / 5.0, -1.0 / 5.0, 8.0 / 315.0, -1.0 / 560.0)


def laplace(padded, extent_x, extent_y, extent_z):
    center = padded[4:4 + extent_x, 4:4 + extent_y, 4:4 + extent_z]
    summed = 3.0 * STENCIL_WEIGHTS[0] * center
    for offset in range(1, 5):
        along = padded[4 + offset:4 + offset + extent_x, 4:4 + extent_y, 4:4 + extent_z]
        along = along + padded[4 - offset:4 - offset + extent_x, 4:4 + extent_y, 4:4 + extent_z]
        along = along + padded[4:4 + extent_x, 4 + offset:4 + offset + extent_y, 4:4 + extent_z]
        along = along + padded[4:4 + extent_x, 4 - offset:4 - offset + extent_y, 4:4 + extent_z]
        along = along + padded[4:4 + extent_x, 4:4 + extent_y, 4 + offset:4 + offset + extent_z]
        along = along + padded[4:4 + extent_x, 4:4 + extent_y, 4 - offset:4 - offset + extent_z]
        summed = summed + STENCIL_WEIGHTS[offset] * along
    return summed


def reference(courant, adjoint_now, adjoint_old, receiver_slab, receiver_cell, residuals, forward_field):
    def one_shot(image_acc, inputs):
        current, previous, slab_ids, cell_ids, trace_rows, snapshots = inputs
        flat_cells = (slab_ids[:, 0] * (CX * NY * NZ) + cell_ids).astype(jnp.int32)
        for step_index in range(STEPS):
            source = jnp.zeros((NX * NY * NZ,), jnp.float32).at[flat_cells].add(trace_rows[step_index])
            source = source.reshape(NX, NY, NZ)
            padded = jnp.pad(current, 4)
            advanced = 2.0 * current - previous + courant * (laplace(padded, NX, NY, NZ) + source)
            image_acc = image_acc + snapshots[step_index].astype(jnp.float32) * advanced
            previous, current = current, advanced
        return image_acc, (current, previous)

    start = jnp.zeros((NX, NY, NZ), jnp.float32)
    image_sum, states = lax.scan(one_shot, start, (adjoint_now, adjoint_old, receiver_slab, receiver_cell, residuals, forward_field))
    return states[0], states[1], image_sum
```

```python
import functools

import jax
import jax.numpy as jnp
from jax import lax
from jax.experimental import pallas as pl
from jax.experimental.pallas import tpu as pltpu
from jax.sharding import PartitionSpec as P

CAP = 48
HALO = 4
PAD = 8
LANES = 128
PACK = 8
MESH = pl.DeviceIdType.MESH
STENCIL_WEIGHTS = (-205.0 / 72.0, 8.0 / 5.0, -1.0 / 5.0, 8.0 / 315.0, -1.0 / 560.0)


def kernel(
    slabs, shots, steps, extent, block_rows,
    slab_ref, cell_ref, res_ref, now_hbm, old_hbm, cour_hbm, fwd_hbm,
    last_hbm, prior_hbm, image_ref,
    ext, old_v, cour_v, fwd_v, last_v, src_v, data_v, pack_v, got_v, img_send, img_recv,
    load_sem, out_sem, halo_send, halo_recv, rec_send, rec_recv, img_ssem, img_rsem,
):
    cx, ny, nz = extent
    rows = ny // shots
    me = lax.axis_index("space")
    shot = lax.axis_index("shot")

    load_now = pltpu.make_async_copy(
        now_hbm.at[0], ext.at[0, pl.ds(HALO, cx), pl.ds(PAD, ny)], load_sem.at[0]
    )
    load_old = pltpu.make_async_copy(old_hbm.at[0], old_v, load_sem.at[1])
    load_cour = pltpu.make_async_copy(cour_hbm, cour_v, load_sem.at[2])
    load_fwd = pltpu.make_async_copy(fwd_hbm.at[0], fwd_v, load_sem.at[3])
    for copy in (load_now, load_old, load_cour, load_fwd):
        copy.start()

    barrier = pltpu.get_barrier_semaphore()
    for delta in range(1, slabs):
        pl.semaphore_signal(
            barrier, inc=1, device_id=(shot, lax.rem(me + delta, slabs)), device_id_type=MESH
        )
    for delta in range(1, shots):
        pl.semaphore_signal(
            barrier, inc=1, device_id=(lax.rem(shot + delta, shots), me), device_id_type=MESH
        )
    pl.semaphore_wait(barrier, slabs - 1 + shots - 1)

    def first_row(i):
        return pl.multiple_of(lax.rem(shot + 1 + i, shots) * rows, rows)

    def halo_copy(step, i, side):
        at = first_row(i)
        if step == 0:
            source = now_hbm.at[0, :, pl.ds(at, rows)]
        else:
            source = ext.at[step, pl.ds(HALO, cx), pl.ds(at + PAD, rows)]
        low_at = HALO + cx if side == 0 else 0
        return pltpu.make_async_remote_copy(
            src_ref=source,
            dst_ref=ext.at[step, pl.ds(low_at, HALO), pl.ds(at + PAD, rows)],
            send_sem=halo_send.at[step, side, i],
            recv_sem=halo_recv.at[step, side, i],
            device_id=(shot, me - 1 if side == 0 else me + 1),
            device_id_type=MESH,
        )

    has_low, has_high = me > 0, me < slabs - 1

    def send_halo(step, i):
        @pl.when(has_low)
        def _():
            halo_copy(step, i, 0).start()

        @pl.when(has_high)
        def _():
            halo_copy(step, i, 1).start()

    def wait_halo(step, i):
        @pl.when(has_high)
        def _():
            halo_copy(step, i, 0).wait_recv()

        @pl.when(has_low)
        def _():
            halo_copy(step, i, 1).wait_recv()

    def wait_sent(step, i):
        @pl.when(has_low)
        def _():
            halo_copy(step, i, 0).wait_send()

        @pl.when(has_high)
        def _():
            halo_copy(step, i, 1).wait_send()

    def loop(count, body):
        lax.fori_loop(0, count, lambda i, c: (body(i), c)[1], 0)

    count = slab_ref.shape[1]
    row = slab_ref[...]
    cells = cell_ref[...]
    first = lax.broadcasted_iota(jnp.int32, (count, count), 0)
    second = lax.broadcasted_iota(jnp.int32, (count, count), 1)
    column = jnp.sum(jnp.where(first == second, row, 0), axis=1, keepdims=True)
    earlier = jnp.where((column == row) & (first < second), 1, 0)
    rank = jnp.sum(earlier, axis=0, keepdims=True)
    lane = rank + lax.rem(me, 2) * CAP
    data_v[...] = jnp.zeros_like(data_v)
    data_v[0:steps] = res_ref[0]
    data_v[steps : steps + 1] = lax.div(cells, nz).astype(jnp.float32)
    data_v[steps + 1 : steps + 2] = lax.rem(cells, nz).astype(jnp.float32)
    slots = lax.broadcasted_iota(jnp.int32, (LANES, count), 0)

    def pack(d):
        onehot = jnp.where((slots == lane) & (row == d), 1.0, 0.0)
        pack_v[d] = lax.dot_general(
            data_v[...], onehot, (((1,), (1,)), ((), ())),
            precision=lax.Precision.HIGHEST, preferred_element_type=jnp.float32,
        )

    def rec_copy(delta):
        to = lax.rem(me + delta, slabs)
        return pltpu.make_async_remote_copy(
            src_ref=pack_v.at[to], dst_ref=got_v.at[me],
            send_sem=rec_send.at[to], recv_sem=rec_recv.at[me],
            device_id=(shot, to), device_id_type=MESH,
        )

    def rec_arrival(delta):
        source = lax.rem(me + delta, slabs)
        return pltpu.make_async_remote_copy(
            src_ref=pack_v.at[source], dst_ref=got_v.at[source],
            send_sem=rec_send.at[source], recv_sem=rec_recv.at[source],
            device_id=(shot, source), device_id_type=MESH,
        )

    send_halo(0, 0)
    loop(slabs, pack)
    for delta in range(1, slabs):
        rec_copy(delta).start()
    loop(shots - 1, lambda i: send_halo(0, i + 1))
    got_v[me] = pack_v[me]

    edge = jnp.zeros((cx, PAD, nz), jnp.float32)
    for step in range(steps):
        ext[step, HALO : HALO + cx, 0:PAD] = edge
        ext[step, HALO : HALO + cx, PAD + ny :] = edge

    def clear(low_at):
        for step in range(steps):
            for layer in range(HALO):
                ext[step, low_at + layer] = jnp.zeros((ny + 2 * PAD, nz), jnp.float32)

    @pl.when(me == 0)
    def _():
        clear(0)

    @pl.when(me == slabs - 1)
    def _():
        clear(HALO + cx)

    for delta in range(1, slabs):
        rec_arrival(delta).wait_recv()
    flat = cx * ny
    group = 4
    for step in range(steps):
        src_v[step] = jnp.zeros((flat, nz), jnp.float32)

    def add_sources(g):
        held = jnp.concatenate(
            [got_v[g * group] + got_v[g * group + 1], got_v[g * group + 2] + got_v[g * group + 3]], axis=1
        )
        where_row = held[steps : steps + 1].astype(jnp.int32)
        where_lane = held[steps + 1 : steps + 2].astype(jnp.int32)
        width = held.shape[1]
        picks = jnp.where(
            lax.broadcasted_iota(jnp.int32, (flat, width), 0) == where_row, 1.0, 0.0
        ).astype(jnp.bfloat16)
        hits = lax.broadcasted_iota(jnp.int32, (nz, width), 0) == where_lane
        for step in range(steps):
            rest = jnp.where(hits, held[step : step + 1], 0.0)
            total = None
            for _ in range(3):
                piece = rest.astype(jnp.bfloat16)
                rest = rest - piece.astype(jnp.float32)
                term = lax.dot_general(
                    picks, piece, (((1,), (1,)), ((), ())), preferred_element_type=jnp.float32
                )
                total = term if total is None else total + term
            src_v[step] += total

    loop(slabs // group, add_sources)
    for copy in (load_now, load_old, load_cour, load_fwd):
        copy.wait()

    def img_copy(i):
        return pltpu.make_async_remote_copy(
            src_ref=img_send.at[i], dst_ref=img_recv.at[i],
            send_sem=img_ssem.at[i], recv_sem=img_rsem.at[i],
            device_id=(lax.rem(shot + 1 + i, shots), me), device_id_type=MESH,
        )

    def out_copy(which, i):
        at = first_row(i)
        if which == 0:
            return pltpu.make_async_copy(
                last_v.at[:, pl.ds(at, rows)], last_hbm.at[0, :, pl.ds(at, rows)], out_sem.at[0, i]
            )
        return pltpu.make_async_copy(
            ext.at[steps - 1, pl.ds(HALO, cx), pl.ds(at + PAD, rows)],
            prior_hbm.at[0, :, pl.ds(at, rows)], out_sem.at[1, i],
        )

    z_at = lax.broadcasted_iota(jnp.int32, (block_rows, nz), 1)

    def update(step, i):
        start = first_row(i)

        def block(b):
            at = pl.multiple_of(start + b * block_rows, block_rows)
            for x in range(cx):
                center = ext[step, HALO + x, pl.ds(at + PAD, block_rows), :]
                summed = (3.0 * STENCIL_WEIGHTS[0]) * center
                for k in range(1, 5):
                    along = ext[step, HALO + x + k, pl.ds(at + PAD, block_rows), :]
                    along += ext[step, HALO + x - k, pl.ds(at + PAD, block_rows), :]
                    along += ext[step, HALO + x, pl.ds(at + PAD + k, block_rows), :]
                    along += ext[step, HALO + x, pl.ds(at + PAD - k, block_rows), :]
                    along += jnp.where(z_at < nz - k, pltpu.roll(center, nz - k, 1), 0.0)
                    along += jnp.where(z_at >= k, pltpu.roll(center, k, 1), 0.0)
                    summed += STENCIL_WEIGHTS[k] * along
                if step == 0:
                    before = old_v[x, pl.ds(at, block_rows), :]
                else:
                    before = ext[step - 1, HALO + x, pl.ds(at + PAD, block_rows), :]
                source = src_v[step, pl.ds(pl.multiple_of(x * ny + at, block_rows), block_rows), :]
                speed = cour_v[x, pl.ds(at, block_rows), :]
                fresh = 2.0 * center - before + speed * (summed + source)
                if step < steps - 1:
                    ext[step + 1, HALO + x, pl.ds(at + PAD, block_rows), :] = fresh
                else:
                    last_v[x, pl.ds(at, block_rows), :] = fresh
                    image = fwd_v[steps - 1, x, pl.ds(at, block_rows), :].astype(jnp.float32) * fresh
                    for s in range(steps - 1):
                        field = ext[s + 1, HALO + x, pl.ds(at + PAD, block_rows), :]
                        image += fwd_v[s, x, pl.ds(at, block_rows), :].astype(jnp.float32) * field
                    img_send[i, x, pl.ds(pl.multiple_of(b * block_rows, block_rows), block_rows), :] = image

        loop(rows // block_rows, block)

    for step in range(steps):

        def chunk(i, step=step):
            wait_halo(step, i)
            update(step, i)
            if step < steps - 1:
                send_halo(step + 1, i)
            if step == steps - 2:
                out_copy(1, i).start()
            if step == steps - 1:
                out_copy(0, i).start()

                @pl.when(i < shots - 1)
                def _():
                    img_copy(i).start()

        loop(shots, chunk)

    for i in range(shots - 1):
        img_copy(i).wait_recv()
    for x in range(cx):
        total = img_send[shots - 1, x]
        for i in range(shots - 1):
            total += img_recv[i, x]
        image_ref[x] = total

    for step in range(steps):
        loop(shots, lambda i, step=step: wait_sent(step, i))
    for delta in range(1, slabs):
        rec_copy(delta).wait_send()
    for i in range(shots - 1):
        img_copy(i).wait_send()
    loop(shots, lambda i: (out_copy(0, i).wait(), out_copy(1, i).wait()))


def solution(mesh):
    slabs, shots = mesh.shape["space"], mesh.shape["shot"]

    def local(courant, now, old, receiver_slab, receiver_cell, residuals, forward):
        cx, ny, nz = courant.shape
        steps = residuals.shape[1]
        rows = ny // shots
        block_rows = min(16, rows)
        anywhere = pl.BlockSpec(memory_space=pl.ANY)
        vmem = pl.BlockSpec(memory_space=pltpu.VMEM)
        f32 = jnp.float32
        dma = pltpu.SemaphoreType.DMA
        return pl.pallas_call(
            functools.partial(kernel, slabs, shots, steps, (cx, ny, nz), block_rows),
            out_shape=(
                jax.ShapeDtypeStruct(now.shape, f32),
                jax.ShapeDtypeStruct(now.shape, f32),
                jax.ShapeDtypeStruct((cx, rows, nz), f32),
            ),
            in_specs=[vmem] * 3 + [anywhere] * 4,
            out_specs=(anywhere, anywhere, vmem),
            scratch_shapes=[
                pltpu.VMEM((steps, cx + 2 * HALO, ny + 2 * PAD, nz), f32),
                pltpu.VMEM((cx, ny, nz), f32),
                pltpu.VMEM((cx, ny, nz), f32),
                pltpu.VMEM(forward.shape[1:], forward.dtype),
                pltpu.VMEM((cx, ny, nz), f32),
                pltpu.VMEM((steps, cx * ny, nz), f32),
                pltpu.VMEM((PACK, receiver_cell.shape[1]), f32),
                pltpu.VMEM((slabs, PACK, LANES), f32),
                pltpu.VMEM((slabs, PACK, LANES), f32),
                pltpu.VMEM((shots, cx, rows, nz), f32),
                pltpu.VMEM((shots, cx, rows, nz), f32),
                dma((4,)),
                dma((2, shots)),
                dma((steps, 2, shots)),
                dma((steps, 2, shots)),
                dma((slabs,)),
                dma((slabs,)),
                dma((shots,)),
                dma((shots,)),
            ],
            compiler_params=pltpu.CompilerParams(
                collective_id=0, has_side_effects=True, vmem_limit_bytes=48 * 1024 * 1024
            ),
        )(receiver_slab.reshape(receiver_cell.shape), receiver_cell, residuals, now, old, courant, forward)

    in_specs = (
        P("space", None, None),
        P("shot", "space", None, None),
        P("shot", "space", None, None),
        P("shot", "space", None),
        P("shot", "space"),
        P("shot", None, "space"),
        P("shot", None, "space", None, None),
    )
    out_specs = (
        P("shot", "space", None, None),
        P("shot", "space", None, None),
        P("space", "shot", None),
    )
    return jax.shard_map(local, mesh=mesh, in_specs=in_specs, out_specs=out_specs, check_vma=False)
```

```python
import functools

import jax
import jax.numpy as jnp
from jax import lax
from jax.experimental import pallas as pl
from jax.experimental.pallas import tpu as pltpu
from jax.sharding import PartitionSpec as P

CAP = 48
HALO = 4
PAD = 8
LANES = 128
VMEM_BYTES = 62 * 1024 * 1024
PACK = 8
MESH = pl.DeviceIdType.MESH
STENCIL_WEIGHTS = (-205.0 / 72.0, 8.0 / 5.0, -1.0 / 5.0, 8.0 / 315.0, -1.0 / 560.0)


def kernel(
    slabs, shots, steps, extent, block_rows,
    slab_hbm, cell_hbm, res_hbm, now_hbm, old_hbm, cour_hbm, fwd_hbm,
    last_hbm, prior_hbm, image_hbm,
    slab_ref, cell_ref, res_ref, ext, old_v, cour_v, fwd_v, last_v, src_v, data_v, pack_v, got_v, img_send, img_recv, image_ref, relay_v,
    load_sem, out_sem, halo_send, halo_recv, rec_send, rec_recv, img_ssem, img_rsem,
    diag_send, diag_recv, relay_send, relay_recv,
):
    cx, ny, nz = extent
    rows = ny // shots
    me = lax.axis_index("space")
    shot = lax.axis_index("shot")

    load_now = pltpu.make_async_copy(
        now_hbm.at[0], ext.at[0, pl.ds(HALO, cx), pl.ds(PAD, ny)], load_sem.at[0]
    )
    load_old = pltpu.make_async_copy(old_hbm.at[0], old_v, load_sem.at[1])
    load_cour = pltpu.make_async_copy(cour_hbm, cour_v, load_sem.at[2])
    load_fwd = pltpu.make_async_copy(fwd_hbm.at[0], fwd_v, load_sem.at[3])
    small_loads = [
        pltpu.make_async_copy(source, target, load_sem.at[4 + at])
        for at, (source, target) in enumerate(
            ((slab_hbm, slab_ref), (cell_hbm, cell_ref), (res_hbm, res_ref))
        )
    ]
    for copy in (*small_loads, load_now, load_old, load_cour, load_fwd):
        copy.start()

    barrier = pltpu.get_barrier_semaphore()
    for delta in range(1, slabs):
        pl.semaphore_signal(
            barrier, inc=1, device_id=(shot, lax.rem(me + delta, slabs)), device_id_type=MESH
        )
    for delta in range(1, shots):
        pl.semaphore_signal(
            barrier, inc=1, device_id=(lax.rem(shot + delta, shots), me), device_id_type=MESH
        )
    pl.semaphore_wait(barrier, slabs - 1 + shots - 1)

    def first_row(i):
        return pl.multiple_of(lax.rem(shot + 1 + i, shots) * rows, rows)

    def halo_copy(step, i, side):
        at = first_row(i)
        if step == 0:
            source = now_hbm.at[0, :, pl.ds(at, rows)]
        else:
            source = ext.at[step, pl.ds(HALO, cx), pl.ds(at + PAD, rows)]
        low_at = HALO + cx if side == 0 else 0
        return pltpu.make_async_remote_copy(
            src_ref=source,
            dst_ref=ext.at[step, pl.ds(low_at, HALO), pl.ds(at + PAD, rows)],
            send_sem=halo_send.at[step, side, i],
            recv_sem=halo_recv.at[step, side, i],
            device_id=(shot, me - 1 if side == 0 else me + 1),
            device_id_type=MESH,
        )

    quad = slabs % 4 == 0 and cx % 2 == 0
    half = cx // 2
    turn = lax.rem(me, 4)
    has_low, has_high = me > 0, me < slabs - 1
    if quad:
        diag_low, diag_high = has_low & (turn == 0), has_high & (turn == 3)
        near_low, near_high = has_low & (turn != 0), has_high & (turn != 3)
        relay_lower, relay_upper = (turn == 0) & (me + 4 < slabs), (turn == 3) & (me >= 7)
    else:
        near_low, near_high = has_low, has_high

    def diag_copy(step, i, up, h):
        at = first_row(i)
        if step == 0:
            source = now_hbm.at[0, pl.ds(h * half, half), pl.ds(at, rows)]
        else:
            source = ext.at[step, pl.ds(HALO + h * half, half), pl.ds(at + PAD, rows)]
        lower = me - 3 if up else me - 4
        return pltpu.make_async_remote_copy(
            src_ref=source,
            dst_ref=relay_v.at[step * shots + i, 0 if up else 1],
            send_sem=diag_send.at[step, h, i],
            recv_sem=relay_recv.at[step * shots + i, 0 if up else 1],
            device_id=(shot, lower + 7 * h),
            device_id_type=MESH,
        )

    def relay_copy(g, up, h):
        step, i = lax.div(g, shots), lax.rem(g, shots)
        low_at = (0 if up else HALO + cx) + h * half
        to = (me + 4 if up else me + 3) - 7 * h
        return pltpu.make_async_remote_copy(
            src_ref=relay_v.at[g, 0 if up else 1],
            dst_ref=ext.at[step, pl.ds(low_at, half), pl.ds(first_row(i) + PAD, rows)],
            send_sem=relay_send.at[g, 0 if up else 1],
            recv_sem=diag_recv.at[step, h, i],
            device_id=(shot, to),
            device_id_type=MESH,
        )

    def relay_arrival(g, up):
        slot = relay_v.at[g, 0 if up else 1]
        return pltpu.make_async_remote_copy(
            src_ref=slot, dst_ref=slot,
            send_sem=relay_send.at[g, 0 if up else 1],
            recv_sem=relay_recv.at[g, 0 if up else 1],
            device_id=(shot, me), device_id_type=MESH,
        )

    def forward(g):
        if quad:
            for h, here in ((0, relay_lower), (1, relay_upper)):

                @pl.when(here)
                def _(h=h):
                    for up in (True, False):
                        relay_arrival(g, up).wait_recv()
                        relay_copy(g, up, h).start()

    def forwarded(g):
        if quad:
            for h, here in ((0, relay_lower), (1, relay_upper)):

                @pl.when(here)
                def _(h=h):
                    for up in (True, False):
                        relay_copy(g, up, h).wait_send()

    def send_halo(step, i):
        if quad:
            for up, here in ((False, diag_low), (True, diag_high)):

                @pl.when(here)
                def _(up=up):
                    for h in range(2):
                        diag_copy(step, i, up, h).start()

        @pl.when(near_low)
        def _():
            halo_copy(step, i, 0).start()

        @pl.when(near_high)
        def _():
            halo_copy(step, i, 1).start()

    def wait_halo(step, i):
        @pl.when(near_high)
        def _():
            halo_copy(step, i, 0).wait_recv()

        @pl.when(near_low)
        def _():
            halo_copy(step, i, 1).wait_recv()

        if quad:
            for up, here in ((True, diag_low), (False, diag_high)):

                @pl.when(here)
                def _(up=up):
                    for h in range(2):
                        low_at = (0 if up else HALO + cx) + h * half
                        slot = ext.at[step, pl.ds(low_at, half), pl.ds(first_row(i) + PAD, rows)]
                        pltpu.make_async_remote_copy(
                            src_ref=slot, dst_ref=slot,
                            send_sem=diag_send.at[step, h, i],
                            recv_sem=diag_recv.at[step, h, i],
                            device_id=(shot, me), device_id_type=MESH,
                        ).wait_recv()

    def wait_sent(step, i):
        if quad:
            for up, here in ((False, diag_low), (True, diag_high)):

                @pl.when(here)
                def _(up=up):
                    for h in range(2):
                        diag_copy(step, i, up, h).wait_send()

        @pl.when(near_low)
        def _():
            halo_copy(step, i, 0).wait_send()

        @pl.when(near_high)
        def _():
            halo_copy(step, i, 1).wait_send()

    def loop(count, body):
        lax.fori_loop(0, count, lambda i, c: (body(i), c)[1], 0)

    send_halo(0, 0)

    for copy in small_loads:
        copy.wait()
    count = slab_ref.shape[1]
    row = slab_ref[...]
    cells = cell_ref[...]
    first = lax.broadcasted_iota(jnp.int32, (count, count), 0)
    second = lax.broadcasted_iota(jnp.int32, (count, count), 1)
    column = jnp.sum(jnp.where(first == second, row, 0), axis=1, keepdims=True)
    earlier = jnp.where((column == row) & (first < second), 1, 0)
    rank = jnp.sum(earlier, axis=0, keepdims=True)
    lane = rank + lax.rem(me, 2) * CAP
    data_v[...] = jnp.zeros_like(data_v)
    for step in range(steps):
        data_v[step : step + 1] = res_ref[step]
    data_v[steps : steps + 1] = lax.div(cells, nz).astype(jnp.float32)
    data_v[steps + 1 : steps + 2] = lax.rem(cells, nz).astype(jnp.float32)
    slots = lax.broadcasted_iota(jnp.int32, (LANES, count), 0)

    def pack(d):
        onehot = jnp.where((slots == lane) & (row == d), 1.0, 0.0)
        pack_v[d] = lax.dot_general(
            data_v[...], onehot, (((1,), (1,)), ((), ())),
            precision=lax.Precision.HIGHEST, preferred_element_type=jnp.float32,
        )

    def rec_copy(delta):
        to = lax.rem(me + delta, slabs)
        return pltpu.make_async_remote_copy(
            src_ref=pack_v.at[to], dst_ref=got_v.at[me],
            send_sem=rec_send.at[to], recv_sem=rec_recv.at[me],
            device_id=(shot, to), device_id_type=MESH,
        )

    def rec_arrival(delta):
        source = lax.rem(me + delta, slabs)
        return pltpu.make_async_remote_copy(
            src_ref=pack_v.at[source], dst_ref=got_v.at[source],
            send_sem=rec_send.at[source], recv_sem=rec_recv.at[source],
            device_id=(shot, source), device_id_type=MESH,
        )

    loop(slabs, pack)
    for delta in range(1, slabs):
        rec_copy(delta).start()
    loop(shots - 1, lambda i: send_halo(0, i + 1))
    got_v[me] = pack_v[me]

    edge = jnp.zeros((cx, PAD, nz), jnp.float32)
    for step in range(steps):
        ext[step, HALO : HALO + cx, 0:PAD] = edge
        ext[step, HALO : HALO + cx, PAD + ny :] = edge

    def clear(low_at):
        for step in range(steps):
            for layer in range(HALO):
                ext[step, low_at + layer] = jnp.zeros((ny + 2 * PAD, nz), jnp.float32)

    @pl.when(me == 0)
    def _():
        clear(0)

    @pl.when(me == slabs - 1)
    def _():
        clear(HALO + cx)

    lead = shots // 2
    forward(0)

    for delta in range(1, slabs):
        rec_arrival(delta).wait_recv()
    flat = cx * ny
    group = 8 if slabs % 8 == 0 else 2
    for step in range(steps):
        src_v[step] = jnp.zeros((flat, nz), jnp.float32)

    def add_sources(g):
        held = jnp.concatenate(
            [got_v[g * group + 2 * p] + got_v[g * group + 2 * p + 1] for p in range(group // 2)], axis=1
        )
        where_row = held[steps : steps + 1].astype(jnp.int32)
        where_lane = held[steps + 1 : steps + 2].astype(jnp.int32)
        width = held.shape[1]
        picks = jnp.where(
            lax.broadcasted_iota(jnp.int32, (flat, width), 0) == where_row, 1.0, 0.0
        ).astype(jnp.bfloat16)
        hits = lax.broadcasted_iota(jnp.int32, (nz, width), 0) == where_lane
        rest = jnp.concatenate(
            [jnp.where(hits, held[step : step + 1], 0.0) for step in range(steps)], axis=0
        )
        total = None
        for _ in range(3):
            piece = rest.astype(jnp.bfloat16)
            rest = rest - piece.astype(jnp.float32)
            term = lax.dot_general(
                picks, piece, (((1,), (1,)), ((), ())), preferred_element_type=jnp.float32
            )
            total = term if total is None else total + term
        for step in range(steps):
            src_v[step] += total[:, step * nz : (step + 1) * nz]

    loop(slabs // group, add_sources)
    for g in range(1, lead):
        forward(g)
    for copy in (load_now, load_old, load_cour, load_fwd):
        copy.wait()

    def img_copy(i):
        return pltpu.make_async_remote_copy(
            src_ref=img_send.at[i], dst_ref=img_recv.at[i],
            send_sem=img_ssem.at[i], recv_sem=img_rsem.at[i],
            device_id=(lax.rem(shot + 1 + i, shots), me), device_id_type=MESH,
        )

    def out_copy(which, i):
        at = first_row(i)
        if which == 0:
            return pltpu.make_async_copy(
                last_v.at[:, pl.ds(at, rows)], last_hbm.at[0, :, pl.ds(at, rows)], out_sem.at[0, i]
            )
        return pltpu.make_async_copy(
            ext.at[steps - 1, pl.ds(HALO, cx), pl.ds(at + PAD, rows)],
            prior_hbm.at[0, :, pl.ds(at, rows)], out_sem.at[1, i],
        )

    z_at = lax.broadcasted_iota(jnp.int32, (block_rows, nz), 1)

    def update(step, i):
        start = first_row(i)

        def block(b):
            at = pl.multiple_of(start + b * block_rows, block_rows)
            for x in range(cx):
                center = ext[step, HALO + x, pl.ds(at + PAD, block_rows), :]
                summed = (3.0 * STENCIL_WEIGHTS[0]) * center
                for k in range(1, 5):
                    along = ext[step, HALO + x + k, pl.ds(at + PAD, block_rows), :]
                    along += ext[step, HALO + x - k, pl.ds(at + PAD, block_rows), :]
                    along += ext[step, HALO + x, pl.ds(at + PAD + k, block_rows), :]
                    along += ext[step, HALO + x, pl.ds(at + PAD - k, block_rows), :]
                    along += jnp.where(z_at < nz - k, pltpu.roll(center, nz - k, 1), 0.0)
                    along += jnp.where(z_at >= k, pltpu.roll(center, k, 1), 0.0)
                    summed += STENCIL_WEIGHTS[k] * along
                if step == 0:
                    before = old_v[x, pl.ds(at, block_rows), :]
                else:
                    before = ext[step - 1, HALO + x, pl.ds(at + PAD, block_rows), :]
                source = src_v[step, pl.ds(pl.multiple_of(x * ny + at, block_rows), block_rows), :]
                speed = cour_v[x, pl.ds(at, block_rows), :]
                fresh = 2.0 * center - before + speed * (summed + source)
                if step < steps - 1:
                    ext[step + 1, HALO + x, pl.ds(at + PAD, block_rows), :] = fresh
                else:
                    last_v[x, pl.ds(at, block_rows), :] = fresh
                    image = fwd_v[steps - 1, x, pl.ds(at, block_rows), :].astype(jnp.float32) * fresh
                    for s in range(steps - 1):
                        field = ext[s + 1, HALO + x, pl.ds(at + PAD, block_rows), :]
                        image += fwd_v[s, x, pl.ds(at, block_rows), :].astype(jnp.float32) * field
                    img_send[i, x, pl.ds(pl.multiple_of(b * block_rows, block_rows), block_rows), :] = image

        loop(rows // block_rows, block)

    for step in range(steps):

        def chunk(i, step=step):
            ahead = step * shots + i + lead

            @pl.when(ahead < steps * shots)
            def _():
                forward(ahead)

            wait_halo(step, i)
            update(step, i)
            if step < steps - 1:
                send_halo(step + 1, i)
            if step == steps - 2:
                out_copy(1, i).start()
            if step == steps - 1:
                out_copy(0, i).start()

                @pl.when(i < shots - 1)
                def _():
                    img_copy(i).start()

        loop(shots, chunk)

    for i in range(shots - 1):
        img_copy(i).wait_recv()
    for x in range(cx):
        total = img_send[shots - 1, x]
        for i in range(shots - 1):
            total += img_recv[i, x]
        image_ref[x] = total
    image_out = pltpu.make_async_copy(image_ref, image_hbm, load_sem.at[7])
    image_out.start()

    for step in range(steps):
        loop(shots, lambda i, step=step: wait_sent(step, i))
    for delta in range(1, slabs):
        rec_copy(delta).wait_send()
    for i in range(shots - 1):
        img_copy(i).wait_send()
    loop(steps * shots, forwarded)
    image_out.wait()
    loop(shots, lambda i: (out_copy(0, i).wait(), out_copy(1, i).wait()))


def store(*refs):
    count = len(refs) // 3
    copies = []
    for at in range(count):
        source, target, sems = refs[at], refs[count + at], refs[2 * count + at]
        for part in range(sems.shape[0]):
            copies.append(pltpu.make_async_copy(source.at[part], target.at[part], sems.at[part]))
    for copy in copies:
        copy.start()
    for copy in copies:
        copy.wait()


def solution(mesh):
    slabs, shots = mesh.shape["space"], mesh.shape["shot"]

    def local(courant, now, old, receiver_slab, receiver_cell, residuals, forward):
        cx, ny, nz = courant.shape
        steps = residuals.shape[1]
        rows = ny // shots
        block_rows = min(16, rows)
        anywhere = pl.BlockSpec(memory_space=pl.ANY)
        f32 = jnp.float32
        dma = pltpu.SemaphoreType.DMA
        hbm = pl.BlockSpec(memory_space=pltpu.HBM)
        parts = pl.pallas_call(
            functools.partial(kernel, slabs, shots, steps, (cx, ny, nz), block_rows),
            out_shape=(
                jax.ShapeDtypeStruct((1, cx, ny, nz), f32),
                jax.ShapeDtypeStruct((1, cx, ny, nz), f32),
                jax.ShapeDtypeStruct((cx, rows, nz), f32),
            ),
            in_specs=[hbm] * 7,
            out_specs=(anywhere,) * 3,
            scratch_shapes=[
                pltpu.VMEM(receiver_cell.shape, jnp.int32),
                pltpu.VMEM(receiver_cell.shape, jnp.int32),
                pltpu.VMEM((steps, 1, receiver_cell.shape[1]), f32),
                pltpu.VMEM((steps, cx + 2 * HALO, ny + 2 * PAD, nz), f32),
                pltpu.VMEM((cx, ny, nz), f32),
                pltpu.VMEM((cx, ny, nz), f32),
                pltpu.VMEM(forward.shape[1:], forward.dtype),
                pltpu.VMEM((cx, ny, nz), f32),
                pltpu.VMEM((steps, cx * ny, nz), f32),
                pltpu.VMEM((PACK, receiver_cell.shape[1]), f32),
                pltpu.VMEM((slabs, PACK, LANES), f32),
                pltpu.VMEM((slabs, PACK, LANES), f32),
                pltpu.VMEM((shots, cx, rows, nz), f32),
                pltpu.VMEM((shots, cx, rows, nz), f32),
                pltpu.VMEM((cx, rows, nz), f32),
                pltpu.VMEM((steps * shots, 2, cx // 2, rows, nz), f32),
                dma((8,)),
                dma((2, shots)),
                dma((steps, 2, shots)),
                dma((steps, 2, shots)),
                dma((slabs,)),
                dma((slabs,)),
                dma((shots,)),
                dma((shots,)),
                dma((steps, 2, shots)),
                dma((steps, 2, shots)),
                dma((steps * shots, 2)),
                dma((steps * shots, 2)),
            ],
            compiler_params=pltpu.CompilerParams(
                collective_id=0, has_side_effects=True, vmem_limit_bytes=VMEM_BYTES
            ),
        )(
            receiver_slab.reshape(receiver_cell.shape), receiver_cell,
            jnp.transpose(residuals, (1, 0, 2)), now, old, courant, forward,
        )
        last, prior = (part.reshape(cx, ny, nz) for part in parts[:2])
        last, prior, image = pl.pallas_call(
            store,
            out_shape=tuple(jax.ShapeDtypeStruct(part.shape, f32) for part in (last, prior, parts[2])),
            in_specs=[anywhere] * 3,
            out_specs=(hbm,) * 3,
            scratch_shapes=[dma((cx,))] * 3,
            compiler_params=pltpu.CompilerParams(vmem_limit_bytes=VMEM_BYTES),
        )(last, prior, parts[2])
        return last[None], prior[None], image

    in_specs = (
        P("space", None, None),
        P("shot", "space", None, None),
        P("shot", "space", None, None),
        P("shot", "space", None),
        P("shot", "space"),
        P("shot", None, "space"),
        P("shot", None, "space", None, None),
    )
    out_specs = (
        P("shot", "space", None, None),
        P("shot", "space", None, None),
        P("space", "shot", None),
    )
    return jax.shard_map(local, mesh=mesh, in_specs=in_specs, out_specs=out_specs, check_vma=False)
```

```python
import functools

import jax
import jax.numpy as jnp
from jax import lax
from jax.experimental import pallas as pl
from jax.experimental.pallas import tpu as pltpu
from jax.sharding import PartitionSpec as P

CAP = 48
HALO = 4
PAD = 8
LANES = 128
VMEM_BYTES = 62 * 1024 * 1024
PACK = 8
MESH = pl.DeviceIdType.MESH
STENCIL_WEIGHTS = (-205.0 / 72.0, 8.0 / 5.0, -1.0 / 5.0, 8.0 / 315.0, -1.0 / 560.0)


def kernel(
    slabs, shots, steps, extent, block_rows,
    slab_hbm, cell_hbm, res_hbm, now_hbm, old_hbm, cour_hbm, fwd_hbm,
    last_hbm, prior_hbm, image_hbm,
    slab_ref, cell_ref, res_ref, ext, old_v, cour_v, fwd_v, last_v, src_v, data_v, pack_v, got_v, img_send, img_recv, image_ref, relay_v,
    load_sem, out_sem, halo_send, halo_recv, rec_send, rec_recv, img_ssem, img_rsem,
    diag_send, diag_recv, relay_send, relay_recv,
):
    cx, ny, nz = extent
    rows = ny // shots
    me = lax.axis_index("space")
    shot = lax.axis_index("shot")

    load_now = pltpu.make_async_copy(
        now_hbm.at[0], ext.at[0, pl.ds(HALO, cx), pl.ds(PAD, ny)], load_sem.at[0]
    )
    load_old = pltpu.make_async_copy(old_hbm.at[0], old_v, load_sem.at[1])
    load_cour = pltpu.make_async_copy(cour_hbm, cour_v, load_sem.at[2])
    load_fwd = pltpu.make_async_copy(fwd_hbm.at[0], fwd_v, load_sem.at[3])
    small_loads = [
        pltpu.make_async_copy(source, target, load_sem.at[4 + at])
        for at, (source, target) in enumerate(
            ((slab_hbm, slab_ref), (cell_hbm, cell_ref), (res_hbm, res_ref))
        )
    ]
    for copy in (*small_loads, load_now, load_old, load_cour, load_fwd):
        copy.start()

    barrier = pltpu.get_barrier_semaphore()
    for delta in range(1, slabs):
        pl.semaphore_signal(
            barrier, inc=1, device_id=(shot, lax.rem(me + delta, slabs)), device_id_type=MESH
        )
    for delta in range(1, shots):
        pl.semaphore_signal(
            barrier, inc=1, device_id=(lax.rem(shot + delta, shots), me), device_id_type=MESH
        )
    pl.semaphore_wait(barrier, slabs - 1 + shots - 1)

    def first_row(i):
        return pl.multiple_of(lax.rem(shot + 1 + i, shots) * rows, rows)

    def halo_copy(step, i, side):
        at = first_row(i)
        if step == 0:
            source = now_hbm.at[0, :, pl.ds(at, rows)]
        else:
            source = ext.at[step, pl.ds(HALO, cx), pl.ds(at + PAD, rows)]
        low_at = HALO + cx if side == 0 else 0
        return pltpu.make_async_remote_copy(
            src_ref=source,
            dst_ref=ext.at[step, pl.ds(low_at, HALO), pl.ds(at + PAD, rows)],
            send_sem=halo_send.at[step, side, i],
            recv_sem=halo_recv.at[step, side, i],
            device_id=(shot, me - 1 if side == 0 else me + 1),
            device_id_type=MESH,
        )

    quad = slabs % 4 == 0 and cx % 2 == 0
    half = cx // 2
    turn = lax.rem(me, 4)
    has_low, has_high = me > 0, me < slabs - 1
    if quad:
        diag_low, diag_high = has_low & (turn == 0), has_high & (turn == 3)
        near_low, near_high = has_low & (turn != 0), has_high & (turn != 3)
        relay_lower, relay_upper = (turn == 0) & (me + 4 < slabs), (turn == 3) & (me >= 7)
    else:
        near_low, near_high = has_low, has_high

    def diag_copy(step, i, up, h):
        at = first_row(i)
        if step == 0:
            source = now_hbm.at[0, pl.ds(h * half, half), pl.ds(at, rows)]
        else:
            source = ext.at[step, pl.ds(HALO + h * half, half), pl.ds(at + PAD, rows)]
        if h == 0:
            target = ext.at[step, pl.ds(0 if up else HALO + cx, half), pl.ds(at + PAD, rows)]
            arrived, to = diag_recv.at[step, 0, i], me + 1 if up else me - 1
        else:
            target = relay_v.at[step * shots + i]
            arrived, to = relay_recv.at[step * shots + i], me + 4 if up else me - 4
        return pltpu.make_async_remote_copy(
            src_ref=source, dst_ref=target, send_sem=diag_send.at[step, h, i], recv_sem=arrived,
            device_id=(shot, to), device_id_type=MESH,
        )

    def relay_copy(g, up):
        step, i = lax.div(g, shots), lax.rem(g, shots)
        low_at = (0 if up else HALO + cx) + half
        return pltpu.make_async_remote_copy(
            src_ref=relay_v.at[g],
            dst_ref=ext.at[step, pl.ds(low_at, half), pl.ds(first_row(i) + PAD, rows)],
            send_sem=relay_send.at[g],
            recv_sem=diag_recv.at[step, 1, i],
            device_id=(shot, me - 3 if up else me + 3),
            device_id_type=MESH,
        )

    def forward(g):
        if quad:
            for up, here in ((False, relay_lower), (True, relay_upper)):

                @pl.when(here)
                def _(up=up):
                    slot = relay_v.at[g]
                    pltpu.make_async_remote_copy(
                        src_ref=slot, dst_ref=slot, send_sem=relay_send.at[g], recv_sem=relay_recv.at[g],
                        device_id=(shot, me), device_id_type=MESH,
                    ).wait_recv()
                    relay_copy(g, up).start()

    def forwarded(g):
        if quad:
            for up, here in ((False, relay_lower), (True, relay_upper)):

                @pl.when(here)
                def _(up=up):
                    relay_copy(g, up).wait_send()

    def send_halo(step, i):
        if quad:
            for up, here in ((False, diag_low), (True, diag_high)):

                @pl.when(here)
                def _(up=up):
                    for h in range(2):
                        diag_copy(step, i, up, h).start()

        @pl.when(near_low)
        def _():
            halo_copy(step, i, 0).start()

        @pl.when(near_high)
        def _():
            halo_copy(step, i, 1).start()

    def wait_halo(step, i):
        @pl.when(near_high)
        def _():
            halo_copy(step, i, 0).wait_recv()

        @pl.when(near_low)
        def _():
            halo_copy(step, i, 1).wait_recv()

        if quad:
            for up, here in ((True, diag_low), (False, diag_high)):

                @pl.when(here)
                def _(up=up):
                    for h in range(2):
                        low_at = (0 if up else HALO + cx) + h * half
                        slot = ext.at[step, pl.ds(low_at, half), pl.ds(first_row(i) + PAD, rows)]
                        pltpu.make_async_remote_copy(
                            src_ref=slot, dst_ref=slot,
                            send_sem=diag_send.at[step, h, i],
                            recv_sem=diag_recv.at[step, h, i],
                            device_id=(shot, me), device_id_type=MESH,
                        ).wait_recv()

    def wait_sent(step, i):
        if quad:
            for up, here in ((False, diag_low), (True, diag_high)):

                @pl.when(here)
                def _(up=up):
                    for h in range(2):
                        diag_copy(step, i, up, h).wait_send()

        @pl.when(near_low)
        def _():
            halo_copy(step, i, 0).wait_send()

        @pl.when(near_high)
        def _():
            halo_copy(step, i, 1).wait_send()

    def loop(count, body):
        lax.fori_loop(0, count, lambda i, c: (body(i), c)[1], 0)

    send_halo(0, 0)

    for copy in small_loads:
        copy.wait()
    count = slab_ref.shape[1]
    row = slab_ref[...]
    cells = cell_ref[...]
    first = lax.broadcasted_iota(jnp.int32, (count, count), 0)
    second = lax.broadcasted_iota(jnp.int32, (count, count), 1)
    column = jnp.sum(jnp.where(first == second, row, 0), axis=1, keepdims=True)
    earlier = jnp.where((column == row) & (first < second), 1, 0)
    rank = jnp.sum(earlier, axis=0, keepdims=True)
    lane = rank + lax.rem(me, 2) * CAP
    data_v[...] = jnp.zeros_like(data_v)
    for step in range(steps):
        data_v[step : step + 1] = res_ref[step]
    data_v[steps : steps + 1] = lax.div(cells, nz).astype(jnp.float32)
    data_v[steps + 1 : steps + 2] = lax.rem(cells, nz).astype(jnp.float32)
    slots = lax.broadcasted_iota(jnp.int32, (LANES, count), 0)
    left, pieces = data_v[...], []
    for _ in range(3):
        pieces.append(left.astype(jnp.bfloat16).astype(jnp.float32))
        left = left - pieces[-1]
    pieces = jnp.concatenate(pieces, axis=0).astype(jnp.bfloat16)

    def pack(d):
        onehot = jnp.where((slots == lane) & (row == d), 1.0, 0.0).astype(jnp.bfloat16)
        packed = lax.dot_general(
            pieces, onehot, (((1,), (1,)), ((), ())), preferred_element_type=jnp.float32
        )
        pack_v[d] = packed[:PACK] + packed[PACK : 2 * PACK] + packed[2 * PACK :]

    def rec_copy(delta):
        to = lax.rem(me + delta, slabs)
        return pltpu.make_async_remote_copy(
            src_ref=pack_v.at[to], dst_ref=got_v.at[me],
            send_sem=rec_send.at[to], recv_sem=rec_recv.at[me],
            device_id=(shot, to), device_id_type=MESH,
        )

    def rec_arrival(delta):
        source = lax.rem(me + delta, slabs)
        return pltpu.make_async_remote_copy(
            src_ref=pack_v.at[source], dst_ref=got_v.at[source],
            send_sem=rec_send.at[source], recv_sem=rec_recv.at[source],
            device_id=(shot, source), device_id_type=MESH,
        )

    loop(slabs, pack)
    for delta in range(1, slabs):
        rec_copy(delta).start()
    loop(shots - 1, lambda i: send_halo(0, i + 1))
    got_v[me] = pack_v[me]

    edge = jnp.zeros((cx, PAD, nz), jnp.float32)
    for step in range(steps):
        ext[step, HALO : HALO + cx, 0:PAD] = edge
        ext[step, HALO : HALO + cx, PAD + ny :] = edge

    def clear(low_at):
        for step in range(steps):
            for layer in range(HALO):
                ext[step, low_at + layer] = jnp.zeros((ny + 2 * PAD, nz), jnp.float32)

    @pl.when(me == 0)
    def _():
        clear(0)

    @pl.when(me == slabs - 1)
    def _():
        clear(HALO + cx)

    lead = shots // 2
    forward(0)

    for delta in range(1, slabs):
        rec_arrival(delta).wait_recv()
    for g in range(1, lead):
        forward(g)
    flat = cx * ny
    group = 8 if slabs % 8 == 0 else 2
    for step in range(steps):
        src_v[step] = jnp.zeros((flat, nz), jnp.float32)

    def add_sources(g):
        held = jnp.concatenate(
            [got_v[g * group + 2 * p] + got_v[g * group + 2 * p + 1] for p in range(group // 2)], axis=1
        )
        where_row = held[steps : steps + 1].astype(jnp.int32)
        where_lane = held[steps + 1 : steps + 2].astype(jnp.int32)
        width = held.shape[1]
        picks = jnp.where(
            lax.broadcasted_iota(jnp.int32, (flat, width), 0) == where_row, 1.0, 0.0
        ).astype(jnp.bfloat16)
        hits = lax.broadcasted_iota(jnp.int32, (nz, width), 0) == where_lane
        rest = jnp.concatenate(
            [jnp.where(hits, held[step : step + 1], 0.0) for step in range(steps)], axis=0
        )
        total = None
        for _ in range(3):
            piece = rest.astype(jnp.bfloat16)
            rest = rest - piece.astype(jnp.float32)
            term = lax.dot_general(
                picks, piece, (((1,), (1,)), ((), ())), preferred_element_type=jnp.float32
            )
            total = term if total is None else total + term
        for step in range(steps):
            src_v[step] += total[:, step * nz : (step + 1) * nz]

    loop(slabs // group, add_sources)
    for copy in (load_now, load_old, load_cour, load_fwd):
        copy.wait()

    def img_copy(i):
        return pltpu.make_async_remote_copy(
            src_ref=img_send.at[i], dst_ref=img_recv.at[i],
            send_sem=img_ssem.at[i], recv_sem=img_rsem.at[i],
            device_id=(lax.rem(shot + 1 + i, shots), me), device_id_type=MESH,
        )

    def out_copy(which, i):
        at = first_row(i)
        if which == 0:
            return pltpu.make_async_copy(
                last_v.at[:, pl.ds(at, rows)], last_hbm.at[0, :, pl.ds(at, rows)], out_sem.at[0, i]
            )
        return pltpu.make_async_copy(
            ext.at[steps - 1, pl.ds(HALO, cx), pl.ds(at + PAD, rows)],
            prior_hbm.at[0, :, pl.ds(at, rows)], out_sem.at[1, i],
        )

    z_at = lax.broadcasted_iota(jnp.int32, (block_rows, nz), 1)

    def update(step, i):
        start = first_row(i)

        def block(b):
            at = pl.multiple_of(start + b * block_rows, block_rows)
            for x in range(cx):
                center = ext[step, HALO + x, pl.ds(at + PAD, block_rows), :]
                summed = (3.0 * STENCIL_WEIGHTS[0]) * center
                for k in range(1, 5):
                    along = ext[step, HALO + x + k, pl.ds(at + PAD, block_rows), :]
                    along += ext[step, HALO + x - k, pl.ds(at + PAD, block_rows), :]
                    along += ext[step, HALO + x, pl.ds(at + PAD + k, block_rows), :]
                    along += ext[step, HALO + x, pl.ds(at + PAD - k, block_rows), :]
                    along += jnp.where(z_at < nz - k, pltpu.roll(center, nz - k, 1), 0.0)
                    along += jnp.where(z_at >= k, pltpu.roll(center, k, 1), 0.0)
                    summed += STENCIL_WEIGHTS[k] * along
                if step == 0:
                    before = old_v[x, pl.ds(at, block_rows), :]
                else:
                    before = ext[step - 1, HALO + x, pl.ds(at + PAD, block_rows), :]
                source = src_v[step, pl.ds(pl.multiple_of(x * ny + at, block_rows), block_rows), :]
                speed = cour_v[x, pl.ds(at, block_rows), :]
                fresh = 2.0 * center - before + speed * (summed + source)
                if step < steps - 1:
                    ext[step + 1, HALO + x, pl.ds(at + PAD, block_rows), :] = fresh
                else:
                    last_v[x, pl.ds(at, block_rows), :] = fresh
                    image = fwd_v[steps - 1, x, pl.ds(at, block_rows), :].astype(jnp.float32) * fresh
                    for s in range(steps - 1):
                        field = ext[s + 1, HALO + x, pl.ds(at + PAD, block_rows), :]
                        image += fwd_v[s, x, pl.ds(at, block_rows), :].astype(jnp.float32) * field
                    img_send[i, x, pl.ds(pl.multiple_of(b * block_rows, block_rows), block_rows), :] = image

        loop(rows // block_rows, block)

    for step in range(steps):

        def chunk(i, step=step):
            ahead = step * shots + i + lead

            @pl.when(ahead < steps * shots)
            def _():
                forward(ahead)

            wait_halo(step, i)
            update(step, i)
            if step < steps - 1:
                send_halo(step + 1, i)
            if step == steps - 2:
                out_copy(1, i).start()
            if step == steps - 1:
                out_copy(0, i).start()

                @pl.when(i < shots - 1)
                def _():
                    img_copy(i).start()

        loop(shots, chunk)

    for i in range(shots - 1):
        img_copy(i).wait_recv()
    for x in range(cx):
        total = img_send[shots - 1, x]
        for i in range(shots - 1):
            total += img_recv[i, x]
        image_ref[x] = total
    image_out = pltpu.make_async_copy(image_ref, image_hbm, load_sem.at[7])
    image_out.start()

    for step in range(steps):
        loop(shots, lambda i, step=step: wait_sent(step, i))
    for delta in range(1, slabs):
        rec_copy(delta).wait_send()
    for i in range(shots - 1):
        img_copy(i).wait_send()
    loop(steps * shots, forwarded)
    image_out.wait()
    loop(shots, lambda i: (out_copy(0, i).wait(), out_copy(1, i).wait()))


def store(count, *refs):
    loads, stores = [], []
    for at in range(count):
        source, target, held, sems = (refs[at + count * kind] for kind in range(4))
        for part in range(held.shape[0]):
            loads.append(pltpu.make_async_copy(source.at[part], held.at[part], sems.at[0, part]))
            stores.append(pltpu.make_async_copy(held.at[part], target.at[part], sems.at[1, part]))
    for load in loads:
        load.start()
    for load, write in zip(loads, stores):
        load.wait()
        write.start()
    for write in stores:
        write.wait()


def solution(mesh):
    slabs, shots = mesh.shape["space"], mesh.shape["shot"]

    def local(courant, now, old, receiver_slab, receiver_cell, residuals, forward):
        cx, ny, nz = courant.shape
        steps = residuals.shape[1]
        rows = ny // shots
        block_rows = min(16, rows)
        anywhere = pl.BlockSpec(memory_space=pl.ANY)
        f32 = jnp.float32
        dma = pltpu.SemaphoreType.DMA
        hbm = pl.BlockSpec(memory_space=pltpu.HBM)
        parts = pl.pallas_call(
            functools.partial(kernel, slabs, shots, steps, (cx, ny, nz), block_rows),
            out_shape=(
                jax.ShapeDtypeStruct((1, cx, ny, nz), f32),
                jax.ShapeDtypeStruct((1, cx, ny, nz), f32),
                jax.ShapeDtypeStruct((cx, rows, nz), f32),
            ),
            in_specs=[hbm] * 7,
            out_specs=(anywhere,) * 3,
            scratch_shapes=[
                pltpu.VMEM(receiver_cell.shape, jnp.int32),
                pltpu.VMEM(receiver_cell.shape, jnp.int32),
                pltpu.VMEM((steps, 1, receiver_cell.shape[1]), f32),
                pltpu.VMEM((steps, cx + 2 * HALO, ny + 2 * PAD, nz), f32),
                pltpu.VMEM((cx, ny, nz), f32),
                pltpu.VMEM((cx, ny, nz), f32),
                pltpu.VMEM(forward.shape[1:], forward.dtype),
                pltpu.VMEM((cx, ny, nz), f32),
                pltpu.VMEM((steps, cx * ny, nz), f32),
                pltpu.VMEM((PACK, receiver_cell.shape[1]), f32),
                pltpu.VMEM((slabs, PACK, LANES), f32),
                pltpu.VMEM((slabs, PACK, LANES), f32),
                pltpu.VMEM((shots, cx, rows, nz), f32),
                pltpu.VMEM((shots, cx, rows, nz), f32),
                pltpu.VMEM((cx, rows, nz), f32),
                pltpu.VMEM((steps * shots, cx // 2, rows, nz), f32),
                dma((8,)),
                dma((2, shots)),
                dma((steps, 2, shots)),
                dma((steps, 2, shots)),
                dma((slabs,)),
                dma((slabs,)),
                dma((shots,)),
                dma((shots,)),
                dma((steps, 2, shots)),
                dma((steps, 2, shots)),
                dma((steps * shots,)),
                dma((steps * shots,)),
            ],
            compiler_params=pltpu.CompilerParams(
                collective_id=0, has_side_effects=True, vmem_limit_bytes=VMEM_BYTES
            ),
        )(
            receiver_slab.reshape(receiver_cell.shape), receiver_cell,
            jnp.transpose(residuals, (1, 0, 2)), now, old, courant, forward,
        )
        last, prior = (part.reshape(cx, ny, nz) for part in parts[:2])
        last, prior, image = pl.pallas_call(
            functools.partial(store, 3),
            out_shape=tuple(jax.ShapeDtypeStruct(part.shape, f32) for part in (last, prior, parts[2])),
            in_specs=[anywhere] * 3,
            out_specs=(hbm,) * 3,
            scratch_shapes=[pltpu.VMEM(part.shape, f32) for part in (last, prior, parts[2])] + [dma((2, cx))] * 3,
            compiler_params=pltpu.CompilerParams(vmem_limit_bytes=VMEM_BYTES),
        )(last, prior, parts[2])
        return last[None], prior[None], image

    in_specs = (
        P("space", None, None),
        P("shot", "space", None, None),
        P("shot", "space", None, None),
        P("shot", "space", None),
        P("shot", "space"),
        P("shot", None, "space"),
        P("shot", None, "space", None, None),
    )
    out_specs = (
        P("shot", "space", None, None),
        P("shot", "space", None, None),
        P("space", "shot", None),
    )
    return jax.shard_map(local, mesh=mesh, in_specs=in_specs, out_specs=out_specs, check_vma=False)
```

```python
import functools

import jax
import jax.numpy as jnp
from jax import lax
from jax.experimental import pallas as pl
from jax.experimental.pallas import tpu as pltpu
from jax.sharding import PartitionSpec as P

CAP = 48
HALO = 4
PAD = 8
LANES = 128
VMEM_BYTES = 62 * 1024 * 1024
PACK = 8
MESH = pl.DeviceIdType.MESH
STENCIL_WEIGHTS = (-205.0 / 72.0, 8.0 / 5.0, -1.0 / 5.0, 8.0 / 315.0, -1.0 / 560.0)


def kernel(
    slabs, shots, steps, extent, block_rows,
    slab_hbm, cell_hbm, res_hbm, now_hbm, old_hbm, cour_hbm, fwd_hbm,
    last_hbm, prior_hbm, image_hbm,
    slab_ref, cell_ref, res_ref, ext, old_v, cour_v, fwd_v, last_v, src_v, data_v, pack_v, got_v, img_send, img_recv, image_ref, relay_v,
    load_sem, out_sem, halo_send, halo_recv, rec_send, rec_recv, img_ssem, img_rsem,
    diag_send, diag_recv, relay_send, relay_recv,
):
    cx, ny, nz = extent
    rows = ny // shots
    me = lax.axis_index("space")
    shot = lax.axis_index("shot")

    load_now = pltpu.make_async_copy(
        now_hbm.at[0], ext.at[0, pl.ds(HALO, cx), pl.ds(PAD, ny)], load_sem.at[0]
    )
    load_old = pltpu.make_async_copy(old_hbm.at[0], old_v, load_sem.at[1])
    load_cour = pltpu.make_async_copy(cour_hbm, cour_v, load_sem.at[2])
    load_fwd = pltpu.make_async_copy(fwd_hbm.at[0], fwd_v, load_sem.at[3])
    small_loads = [
        pltpu.make_async_copy(source, target, load_sem.at[4 + at])
        for at, (source, target) in enumerate(
            ((slab_hbm, slab_ref), (cell_hbm, cell_ref), (res_hbm, res_ref))
        )
    ]
    for copy in (*small_loads, load_now, load_old, load_cour, load_fwd):
        copy.start()

    barrier = pltpu.get_barrier_semaphore()
    for delta in range(1, slabs):
        pl.semaphore_signal(
            barrier, inc=1, device_id=(shot, lax.rem(me + delta, slabs)), device_id_type=MESH
        )
    for delta in range(1, shots):
        pl.semaphore_signal(
            barrier, inc=1, device_id=(lax.rem(shot + delta, shots), me), device_id_type=MESH
        )
    pl.semaphore_wait(barrier, slabs - 1 + shots - 1)

    def first_row(i):
        return pl.multiple_of(lax.rem(shot + 1 + i, shots) * rows, rows)

    def halo_copy(step, i, side):
        at = first_row(i)
        if step == 0:
            source = now_hbm.at[0, :, pl.ds(at, rows)]
        else:
            source = ext.at[step, pl.ds(HALO, cx), pl.ds(at + PAD, rows)]
        low_at = HALO + cx if side == 0 else 0
        return pltpu.make_async_remote_copy(
            src_ref=source,
            dst_ref=ext.at[step, pl.ds(low_at, HALO), pl.ds(at + PAD, rows)],
            send_sem=halo_send.at[step, side, i],
            recv_sem=halo_recv.at[step, side, i],
            device_id=(shot, me - 1 if side == 0 else me + 1),
            device_id_type=MESH,
        )

    quad = slabs % 4 == 0 and cx % 2 == 0
    half = cx // 2
    turn = lax.rem(me, 4)
    has_low, has_high = me > 0, me < slabs - 1
    if quad:
        diag_low, diag_high = has_low & (turn == 0), has_high & (turn == 3)
        near_low, near_high = has_low & (turn != 0), has_high & (turn != 3)
        relay_lower, relay_upper = (turn == 0) & (me + 4 < slabs), (turn == 3) & (me >= 7)
    else:
        near_low, near_high = has_low, has_high

    def diag_copy(step, i, up, h):
        at = first_row(i)
        if step == 0:
            source = now_hbm.at[0, pl.ds(h * half, half), pl.ds(at, rows)]
        else:
            source = ext.at[step, pl.ds(HALO + h * half, half), pl.ds(at + PAD, rows)]
        if h == 0:
            target = ext.at[step, pl.ds(0 if up else HALO + cx, half), pl.ds(at + PAD, rows)]
            arrived, to = diag_recv.at[step, 0, i], me + 1 if up else me - 1
        else:
            target = relay_v.at[step * shots + i]
            arrived, to = relay_recv.at[step * shots + i], me + 4 if up else me - 4
        return pltpu.make_async_remote_copy(
            src_ref=source, dst_ref=target, send_sem=diag_send.at[step, h, i], recv_sem=arrived,
            device_id=(shot, to), device_id_type=MESH,
        )

    def relay_copy(g, up):
        step, i = lax.div(g, shots), lax.rem(g, shots)
        low_at = (0 if up else HALO + cx) + half
        return pltpu.make_async_remote_copy(
            src_ref=relay_v.at[g],
            dst_ref=ext.at[step, pl.ds(low_at, half), pl.ds(first_row(i) + PAD, rows)],
            send_sem=relay_send.at[g],
            recv_sem=diag_recv.at[step, 1, i],
            device_id=(shot, me - 3 if up else me + 3),
            device_id_type=MESH,
        )

    def forward(g):
        if quad:
            for up, here in ((False, relay_lower), (True, relay_upper)):

                @pl.when(here)
                def _(up=up):
                    slot = relay_v.at[g]
                    pltpu.make_async_remote_copy(
                        src_ref=slot, dst_ref=slot, send_sem=relay_send.at[g], recv_sem=relay_recv.at[g],
                        device_id=(shot, me), device_id_type=MESH,
                    ).wait_recv()
                    relay_copy(g, up).start()

    def forwarded(g):
        if quad:
            for up, here in ((False, relay_lower), (True, relay_upper)):

                @pl.when(here)
                def _(up=up):
                    relay_copy(g, up).wait_send()

    def send_halo(step, i):
        if quad:
            for up, here in ((False, diag_low), (True, diag_high)):

                @pl.when(here)
                def _(up=up):
                    for h in range(2):
                        diag_copy(step, i, up, h).start()

        @pl.when(near_low)
        def _():
            halo_copy(step, i, 0).start()

        @pl.when(near_high)
        def _():
            halo_copy(step, i, 1).start()

    def wait_halo(step, i):
        @pl.when(near_high)
        def _():
            halo_copy(step, i, 0).wait_recv()

        @pl.when(near_low)
        def _():
            halo_copy(step, i, 1).wait_recv()

        if quad:
            for up, here in ((True, diag_low), (False, diag_high)):

                @pl.when(here)
                def _(up=up):
                    for h in range(2):
                        low_at = (0 if up else HALO + cx) + h * half
                        slot = ext.at[step, pl.ds(low_at, half), pl.ds(first_row(i) + PAD, rows)]
                        pltpu.make_async_remote_copy(
                            src_ref=slot, dst_ref=slot,
                            send_sem=diag_send.at[step, h, i],
                            recv_sem=diag_recv.at[step, h, i],
                            device_id=(shot, me), device_id_type=MESH,
                        ).wait_recv()

    def wait_sent(step, i):
        if quad:
            for up, here in ((False, diag_low), (True, diag_high)):

                @pl.when(here)
                def _(up=up):
                    for h in range(2):
                        diag_copy(step, i, up, h).wait_send()

        @pl.when(near_low)
        def _():
            halo_copy(step, i, 0).wait_send()

        @pl.when(near_high)
        def _():
            halo_copy(step, i, 1).wait_send()

    def loop(count, body):
        lax.fori_loop(0, count, lambda i, c: (body(i), c)[1], 0)

    send_halo(0, 0)

    for copy in small_loads:
        copy.wait()
    count = slab_ref.shape[1]
    row = slab_ref[...]
    cells = cell_ref[...]
    first = lax.broadcasted_iota(jnp.int32, (count, count), 0)
    second = lax.broadcasted_iota(jnp.int32, (count, count), 1)
    column = jnp.sum(jnp.where(first == second, row, 0), axis=1, keepdims=True)
    earlier = jnp.where((column == row) & (first < second), 1, 0)
    rank = jnp.sum(earlier, axis=0, keepdims=True)
    lane = rank + lax.rem(me, 2) * CAP
    data_v[...] = jnp.zeros_like(data_v)
    for step in range(steps):
        data_v[step : step + 1] = res_ref[step]
    data_v[steps : steps + 1] = lax.div(cells, nz).astype(jnp.float32)
    data_v[steps + 1 : steps + 2] = lax.rem(cells, nz).astype(jnp.float32)
    slots = lax.broadcasted_iota(jnp.int32, (LANES, count), 0)
    left, pieces = data_v[...], []
    for _ in range(3):
        pieces.append(left.astype(jnp.bfloat16).astype(jnp.float32))
        left = left - pieces[-1]
    pieces = jnp.concatenate(pieces, axis=0).astype(jnp.bfloat16)

    def pack(d):
        onehot = jnp.where((slots == lane) & (row == d), 1.0, 0.0).astype(jnp.bfloat16)
        packed = lax.dot_general(
            pieces, onehot, (((1,), (1,)), ((), ())), preferred_element_type=jnp.float32
        )
        pack_v[d] = packed[:PACK] + packed[PACK : 2 * PACK] + packed[2 * PACK :]

    def rec_copy(delta):
        to = lax.rem(me + delta, slabs)
        return pltpu.make_async_remote_copy(
            src_ref=pack_v.at[to], dst_ref=got_v.at[me],
            send_sem=rec_send.at[to], recv_sem=rec_recv.at[me],
            device_id=(shot, to), device_id_type=MESH,
        )

    def rec_arrival(delta):
        source = lax.rem(me + delta, slabs)
        return pltpu.make_async_remote_copy(
            src_ref=pack_v.at[source], dst_ref=got_v.at[source],
            send_sem=rec_send.at[source], recv_sem=rec_recv.at[source],
            device_id=(shot, source), device_id_type=MESH,
        )

    loop(slabs, pack)
    for delta in range(1, slabs):
        rec_copy(delta).start()
    loop(shots - 1, lambda i: send_halo(0, i + 1))
    got_v[me] = pack_v[me]

    edge = jnp.zeros((cx, PAD, nz), jnp.float32)
    for step in range(steps):
        ext[step, HALO : HALO + cx, 0:PAD] = edge
        ext[step, HALO : HALO + cx, PAD + ny :] = edge

    def clear(low_at):
        for step in range(steps):
            for layer in range(HALO):
                ext[step, low_at + layer] = jnp.zeros((ny + 2 * PAD, nz), jnp.float32)

    @pl.when(me == 0)
    def _():
        clear(0)

    @pl.when(me == slabs - 1)
    def _():
        clear(HALO + cx)

    lead = shots // 2
    forward(0)

    for delta in range(1, slabs):
        rec_arrival(delta).wait_recv()
    for g in range(1, lead):
        forward(g)
    flat = cx * ny
    group = 8 if slabs % 8 == 0 else 2
    for step in range(steps):
        src_v[step] = jnp.zeros((flat, nz), jnp.float32)

    def add_sources(g):
        held = jnp.concatenate(
            [got_v[g * group + 2 * p] + got_v[g * group + 2 * p + 1] for p in range(group // 2)], axis=1
        )
        where_row = held[steps : steps + 1].astype(jnp.int32)
        where_lane = held[steps + 1 : steps + 2].astype(jnp.int32)
        width = held.shape[1]
        picks = jnp.where(
            lax.broadcasted_iota(jnp.int32, (flat, width), 0) == where_row, 1.0, 0.0
        ).astype(jnp.bfloat16)
        hits = lax.broadcasted_iota(jnp.int32, (nz, width), 0) == where_lane
        rest = jnp.concatenate(
            [jnp.where(hits, held[step : step + 1], 0.0) for step in range(steps)], axis=0
        )
        total = None
        for _ in range(3):
            piece = rest.astype(jnp.bfloat16)
            rest = rest - piece.astype(jnp.float32)
            term = lax.dot_general(
                picks, piece, (((1,), (1,)), ((), ())), preferred_element_type=jnp.float32
            )
            total = term if total is None else total + term
        for step in range(steps):
            src_v[step] += total[:, step * nz : (step + 1) * nz]

    loop(slabs // group, add_sources)
    for copy in (load_now, load_old, load_cour, load_fwd):
        copy.wait()

    def img_copy(i):
        return pltpu.make_async_remote_copy(
            src_ref=img_send.at[i], dst_ref=img_recv.at[i],
            send_sem=img_ssem.at[i], recv_sem=img_rsem.at[i],
            device_id=(lax.rem(shot + 1 + i, shots), me), device_id_type=MESH,
        )

    def out_copy(which, i):
        at = first_row(i)
        if which == 0:
            return pltpu.make_async_copy(
                last_v.at[:, pl.ds(at, rows)], last_hbm.at[0, :, pl.ds(at, rows)], out_sem.at[0, i]
            )
        return pltpu.make_async_copy(
            ext.at[steps - 1, pl.ds(HALO, cx), pl.ds(at + PAD, rows)],
            prior_hbm.at[0, :, pl.ds(at, rows)], out_sem.at[1, i],
        )

    z_at = lax.broadcasted_iota(jnp.int32, (block_rows, nz), 1)

    def update(step, i):
        start = first_row(i)

        def block(b):
            at = pl.multiple_of(start + b * block_rows, block_rows)
            here = pl.ds(at, block_rows)
            padded = pl.ds(at + PAD, block_rows)
            held = pl.ds(pl.multiple_of(b * block_rows, block_rows), block_rows)
            layers = [ext[step, layer, padded, :] for layer in range(cx + 2 * HALO)]
            fields, images = [], []
            for x in range(cx):
                center = layers[HALO + x]
                summed = (3.0 * STENCIL_WEIGHTS[0]) * center
                for k in range(1, 5):
                    along = layers[HALO + x + k] + layers[HALO + x - k]
                    beside = ext[step, HALO + x, pl.ds(at + PAD + k, block_rows), :]
                    beside += ext[step, HALO + x, pl.ds(at + PAD - k, block_rows), :]
                    deep = jnp.where(z_at < nz - k, pltpu.roll(center, nz - k, 1), 0.0)
                    deep += jnp.where(z_at >= k, pltpu.roll(center, k, 1), 0.0)
                    summed += STENCIL_WEIGHTS[k] * (along + beside + deep)
                if step == 0:
                    before = old_v[x, here, :]
                else:
                    before = ext[step - 1, HALO + x, padded, :]
                source = src_v[step, pl.ds(pl.multiple_of(x * ny + at, block_rows), block_rows), :]
                fresh = 2.0 * center - before + cour_v[x, here, :] * (summed + source)
                image = fwd_v[step, x, here, :].astype(jnp.float32) * fresh
                if step > 0:
                    image += img_send[i, x, held, :]
                fields.append(fresh)
                images.append(image)
            for x in range(cx):
                if step < steps - 1:
                    ext[step + 1, HALO + x, padded, :] = fields[x]
                else:
                    last_v[x, here, :] = fields[x]
                img_send[i, x, held, :] = images[x]

        loop(rows // block_rows, block)

    for step in range(steps):

        def chunk(i, step=step):
            ahead = step * shots + i + lead

            @pl.when(ahead < steps * shots)
            def _():
                forward(ahead)

            wait_halo(step, i)
            update(step, i)
            if step < steps - 1:
                send_halo(step + 1, i)
            if step == steps - 2:
                out_copy(1, i).start()
            if step == steps - 1:
                out_copy(0, i).start()

                @pl.when(i < shots - 1)
                def _():
                    img_copy(i).start()

        loop(shots, chunk)

    for i in range(shots - 1):
        img_copy(i).wait_recv()
    for x in range(cx):
        total = img_send[shots - 1, x]
        for i in range(shots - 1):
            total += img_recv[i, x]
        image_ref[x] = total
    image_out = pltpu.make_async_copy(image_ref, image_hbm, load_sem.at[7])
    image_out.start()

    for step in range(steps):
        loop(shots, lambda i, step=step: wait_sent(step, i))
    for delta in range(1, slabs):
        rec_copy(delta).wait_send()
    for i in range(shots - 1):
        img_copy(i).wait_send()
    loop(steps * shots, forwarded)
    image_out.wait()
    loop(shots, lambda i: (out_copy(0, i).wait(), out_copy(1, i).wait()))


def store(count, *refs):
    loads, stores = [], []
    for at in range(count):
        source, target, held, sems = (refs[at + count * kind] for kind in range(4))
        for part in range(held.shape[0]):
            loads.append(pltpu.make_async_copy(source.at[part], held.at[part], sems.at[0, part]))
            stores.append(pltpu.make_async_copy(held.at[part], target.at[part], sems.at[1, part]))
    for load in loads:
        load.start()
    for load, write in zip(loads, stores):
        load.wait()
        write.start()
    for write in stores:
        write.wait()


def solution(mesh):
    slabs, shots = mesh.shape["space"], mesh.shape["shot"]

    def local(courant, now, old, receiver_slab, receiver_cell, residuals, forward):
        cx, ny, nz = courant.shape
        steps = residuals.shape[1]
        rows = ny // shots
        block_rows = min(32, rows)
        anywhere = pl.BlockSpec(memory_space=pl.ANY)
        f32 = jnp.float32
        dma = pltpu.SemaphoreType.DMA
        hbm = pl.BlockSpec(memory_space=pltpu.HBM)
        parts = pl.pallas_call(
            functools.partial(kernel, slabs, shots, steps, (cx, ny, nz), block_rows),
            out_shape=(
                jax.ShapeDtypeStruct((1, cx, ny, nz), f32),
                jax.ShapeDtypeStruct((1, cx, ny, nz), f32),
                jax.ShapeDtypeStruct((cx, rows, nz), f32),
            ),
            in_specs=[hbm] * 7,
            out_specs=(anywhere,) * 3,
            scratch_shapes=[
                pltpu.VMEM(receiver_cell.shape, jnp.int32),
                pltpu.VMEM(receiver_cell.shape, jnp.int32),
                pltpu.VMEM((steps, 1, receiver_cell.shape[1]), f32),
                pltpu.VMEM((steps, cx + 2 * HALO, ny + 2 * PAD, nz), f32),
                pltpu.VMEM((cx, ny, nz), f32),
                pltpu.VMEM((cx, ny, nz), f32),
                pltpu.VMEM(forward.shape[1:], forward.dtype),
                pltpu.VMEM((cx, ny, nz), f32),
                pltpu.VMEM((steps, cx * ny, nz), f32),
                pltpu.VMEM((PACK, receiver_cell.shape[1]), f32),
                pltpu.VMEM((slabs, PACK, LANES), f32),
                pltpu.VMEM((slabs, PACK, LANES), f32),
                pltpu.VMEM((shots, cx, rows, nz), f32),
                pltpu.VMEM((shots, cx, rows, nz), f32),
                pltpu.VMEM((cx, rows, nz), f32),
                pltpu.VMEM((steps * shots, cx // 2, rows, nz), f32),
                dma((8,)),
                dma((2, shots)),
                dma((steps, 2, shots)),
                dma((steps, 2, shots)),
                dma((slabs,)),
                dma((slabs,)),
                dma((shots,)),
                dma((shots,)),
                dma((steps, 2, shots)),
                dma((steps, 2, shots)),
                dma((steps * shots,)),
                dma((steps * shots,)),
            ],
            compiler_params=pltpu.CompilerParams(
                collective_id=0, has_side_effects=True, vmem_limit_bytes=VMEM_BYTES
            ),
        )(
            receiver_slab.reshape(receiver_cell.shape), receiver_cell,
            jnp.transpose(residuals, (1, 0, 2)), now, old, courant, forward,
        )
        last, prior = (part.reshape(cx, ny, nz) for part in parts[:2])
        last, prior, image = pl.pallas_call(
            functools.partial(store, 3),
            out_shape=tuple(jax.ShapeDtypeStruct(part.shape, f32) for part in (last, prior, parts[2])),
            in_specs=[anywhere] * 3,
            out_specs=(hbm,) * 3,
            scratch_shapes=[pltpu.VMEM(part.shape, f32) for part in (last, prior, parts[2])] + [dma((2, cx))] * 3,
            compiler_params=pltpu.CompilerParams(vmem_limit_bytes=VMEM_BYTES),
        )(last, prior, parts[2])
        return last[None], prior[None], image

    in_specs = (
        P("space", None, None),
        P("shot", "space", None, None),
        P("shot", "space", None, None),
        P("shot", "space", None),
        P("shot", "space"),
        P("shot", None, "space"),
        P("shot", None, "space", None, None),
    )
    out_specs = (
        P("shot", "space", None, None),
        P("shot", "space", None, None),
        P("space", "shot", None),
    )
    return jax.shard_map(local, mesh=mesh, in_specs=in_specs, out_specs=out_specs, check_vma=False)
```

```python
import functools

import jax
import jax.numpy as jnp
from jax import lax
from jax.experimental import pallas as pl
from jax.experimental.pallas import tpu as pltpu
from jax.sharding import PartitionSpec as P

CAP = 48
HALO = 4
PAD = 8
LANES = 128
VMEM_BYTES = 62 * 1024 * 1024
PACK = 8
MESH = pl.DeviceIdType.MESH
STENCIL_WEIGHTS = (-205.0 / 72.0, 8.0 / 5.0, -1.0 / 5.0, 8.0 / 315.0, -1.0 / 560.0)


def kernel(
    slabs, shots, steps, extent, block_rows,
    slab_hbm, cell_hbm, res_hbm, now_hbm, old_hbm, cour_hbm, fwd_hbm,
    last_hbm, prior_hbm, image_hbm,
    slab_ref, cell_ref, res_ref, ext, old_v, cour_v, fwd_v, last_v, src_v, held_v, piece_v, data_v, pack_v, got_v, img_send, img_recv, image_ref, relay_v,
    load_sem, out_sem, halo_send, halo_recv, rec_send, rec_recv, img_ssem, img_rsem,
    diag_send, diag_recv, relay_send, relay_recv,
):
    cx, ny, nz = extent
    rows = ny // shots
    me = lax.axis_index("space")
    shot = lax.axis_index("shot")

    load_now = pltpu.make_async_copy(
        now_hbm.at[0], ext.at[0, pl.ds(HALO, cx), pl.ds(PAD, ny)], load_sem.at[0]
    )
    load_old = pltpu.make_async_copy(old_hbm.at[0], old_v, load_sem.at[1])
    load_cour = pltpu.make_async_copy(cour_hbm, cour_v, load_sem.at[2])
    load_fwd = pltpu.make_async_copy(fwd_hbm.at[0], fwd_v, load_sem.at[3])
    small_loads = [
        pltpu.make_async_copy(source, target, load_sem.at[4 + at])
        for at, (source, target) in enumerate(
            ((slab_hbm, slab_ref), (cell_hbm, cell_ref), (res_hbm, res_ref))
        )
    ]
    for copy in (*small_loads, load_now, load_old, load_cour, load_fwd):
        copy.start()

    barrier = pltpu.get_barrier_semaphore()
    for delta in range(1, slabs):
        pl.semaphore_signal(
            barrier, inc=1, device_id=(shot, lax.rem(me + delta, slabs)), device_id_type=MESH
        )
    for delta in range(1, shots):
        pl.semaphore_signal(
            barrier, inc=1, device_id=(lax.rem(shot + delta, shots), me), device_id_type=MESH
        )
    pl.semaphore_wait(barrier, slabs - 1 + shots - 1)

    def first_row(i):
        return pl.multiple_of(lax.rem(shot + 1 + i, shots) * rows, rows)

    def halo_copy(step, i, side):
        at = first_row(i)
        if step == 0:
            source = now_hbm.at[0, :, pl.ds(at, rows)]
        else:
            source = ext.at[step, pl.ds(HALO, cx), pl.ds(at + PAD, rows)]
        low_at = HALO + cx if side == 0 else 0
        return pltpu.make_async_remote_copy(
            src_ref=source,
            dst_ref=ext.at[step, pl.ds(low_at, HALO), pl.ds(at + PAD, rows)],
            send_sem=halo_send.at[step, side, i],
            recv_sem=halo_recv.at[step, side, i],
            device_id=(shot, me - 1 if side == 0 else me + 1),
            device_id_type=MESH,
        )

    quad = slabs % 4 == 0 and cx % 2 == 0
    half = cx // 2
    turn = lax.rem(me, 4)
    has_low, has_high = me > 0, me < slabs - 1
    if quad:
        diag_low, diag_high = has_low & (turn == 0), has_high & (turn == 3)
        near_low, near_high = has_low & (turn != 0), has_high & (turn != 3)
        relay_lower, relay_upper = (turn == 0) & (me + 4 < slabs), (turn == 3) & (me >= 7)
    else:
        near_low, near_high = has_low, has_high

    def diag_copy(step, i, up, h):
        at = first_row(i)
        if step == 0:
            source = now_hbm.at[0, pl.ds(h * half, half), pl.ds(at, rows)]
        else:
            source = ext.at[step, pl.ds(HALO + h * half, half), pl.ds(at + PAD, rows)]
        if h == 0:
            target = ext.at[step, pl.ds(0 if up else HALO + cx, half), pl.ds(at + PAD, rows)]
            arrived, to = diag_recv.at[step, 0, i], me + 1 if up else me - 1
        else:
            target = relay_v.at[step * shots + i]
            arrived, to = relay_recv.at[step * shots + i], me + 4 if up else me - 4
        return pltpu.make_async_remote_copy(
            src_ref=source, dst_ref=target, send_sem=diag_send.at[step, h, i], recv_sem=arrived,
            device_id=(shot, to), device_id_type=MESH,
        )

    def relay_copy(g, up):
        step, i = lax.div(g, shots), lax.rem(g, shots)
        low_at = (0 if up else HALO + cx) + half
        return pltpu.make_async_remote_copy(
            src_ref=relay_v.at[g],
            dst_ref=ext.at[step, pl.ds(low_at, half), pl.ds(first_row(i) + PAD, rows)],
            send_sem=relay_send.at[g],
            recv_sem=diag_recv.at[step, 1, i],
            device_id=(shot, me - 3 if up else me + 3),
            device_id_type=MESH,
        )

    def forward(g):
        if quad:
            for up, here in ((False, relay_lower), (True, relay_upper)):

                @pl.when(here)
                def _(up=up):
                    slot = relay_v.at[g]
                    pltpu.make_async_remote_copy(
                        src_ref=slot, dst_ref=slot, send_sem=relay_send.at[g], recv_sem=relay_recv.at[g],
                        device_id=(shot, me), device_id_type=MESH,
                    ).wait_recv()
                    relay_copy(g, up).start()

    def forwarded(g):
        if quad:
            for up, here in ((False, relay_lower), (True, relay_upper)):

                @pl.when(here)
                def _(up=up):
                    relay_copy(g, up).wait_send()

    def send_halo(step, i):
        if quad:
            for up, here in ((False, diag_low), (True, diag_high)):

                @pl.when(here)
                def _(up=up):
                    for h in range(2):
                        diag_copy(step, i, up, h).start()

        @pl.when(near_low)
        def _():
            halo_copy(step, i, 0).start()

        @pl.when(near_high)
        def _():
            halo_copy(step, i, 1).start()

    def wait_halo(step, i):
        @pl.when(near_high)
        def _():
            halo_copy(step, i, 0).wait_recv()

        @pl.when(near_low)
        def _():
            halo_copy(step, i, 1).wait_recv()

        if quad:
            for up, here in ((True, diag_low), (False, diag_high)):

                @pl.when(here)
                def _(up=up):
                    for h in range(2):
                        low_at = (0 if up else HALO + cx) + h * half
                        slot = ext.at[step, pl.ds(low_at, half), pl.ds(first_row(i) + PAD, rows)]
                        pltpu.make_async_remote_copy(
                            src_ref=slot, dst_ref=slot,
                            send_sem=diag_send.at[step, h, i],
                            recv_sem=diag_recv.at[step, h, i],
                            device_id=(shot, me), device_id_type=MESH,
                        ).wait_recv()

    def wait_sent(step, i):
        if quad:
            for up, here in ((False, diag_low), (True, diag_high)):

                @pl.when(here)
                def _(up=up):
                    for h in range(2):
                        diag_copy(step, i, up, h).wait_send()

        @pl.when(near_low)
        def _():
            halo_copy(step, i, 0).wait_send()

        @pl.when(near_high)
        def _():
            halo_copy(step, i, 1).wait_send()

    def loop(count, body):
        lax.fori_loop(0, count, lambda i, c: (body(i), c)[1], 0)

    send_halo(0, 0)

    for copy in small_loads:
        copy.wait()
    count = slab_ref.shape[1]
    row = slab_ref[...]
    cells = cell_ref[...]
    first = lax.broadcasted_iota(jnp.int32, (count, count), 0)
    second = lax.broadcasted_iota(jnp.int32, (count, count), 1)
    column = jnp.sum(jnp.where(first == second, row, 0), axis=1, keepdims=True)
    earlier = jnp.where((column == row) & (first < second), 1, 0)
    rank = jnp.sum(earlier, axis=0, keepdims=True)
    lane = rank + lax.rem(me, 2) * CAP
    data_v[...] = jnp.zeros_like(data_v)
    for step in range(steps):
        data_v[step : step + 1] = res_ref[step]
    data_v[steps : steps + 1] = lax.div(cells, nz).astype(jnp.float32)
    data_v[steps + 1 : steps + 2] = lax.rem(cells, nz).astype(jnp.float32)
    slots = lax.broadcasted_iota(jnp.int32, (LANES, count), 0)
    left, pieces = data_v[...], []
    for _ in range(3):
        pieces.append(left.astype(jnp.bfloat16).astype(jnp.float32))
        left = left - pieces[-1]
    pieces = jnp.concatenate(pieces, axis=0).astype(jnp.bfloat16)

    def pack(d):
        onehot = jnp.where((slots == lane) & (row == d), 1.0, 0.0).astype(jnp.bfloat16)
        packed = lax.dot_general(
            pieces, onehot, (((1,), (1,)), ((), ())), preferred_element_type=jnp.float32
        )
        pack_v[d] = packed[:PACK] + packed[PACK : 2 * PACK] + packed[2 * PACK :]

    def rec_copy(delta):
        to = lax.rem(me + delta, slabs)
        return pltpu.make_async_remote_copy(
            src_ref=pack_v.at[to], dst_ref=got_v.at[me],
            send_sem=rec_send.at[to], recv_sem=rec_recv.at[me],
            device_id=(shot, to), device_id_type=MESH,
        )

    def rec_arrival(delta):
        source = lax.rem(me + delta, slabs)
        return pltpu.make_async_remote_copy(
            src_ref=pack_v.at[source], dst_ref=got_v.at[source],
            send_sem=rec_send.at[source], recv_sem=rec_recv.at[source],
            device_id=(shot, source), device_id_type=MESH,
        )

    loop(slabs, pack)
    for delta in range(1, slabs):
        rec_copy(delta).start()
    loop(shots - 1, lambda i: send_halo(0, i + 1))
    got_v[me] = pack_v[me]

    edge = jnp.zeros((cx, PAD, nz), jnp.float32)
    for step in range(steps):
        ext[step, HALO : HALO + cx, 0:PAD] = edge
        ext[step, HALO : HALO + cx, PAD + ny :] = edge

    def clear(low_at):
        for step in range(steps):
            for layer in range(HALO):
                ext[step, low_at + layer] = jnp.zeros((ny + 2 * PAD, nz), jnp.float32)

    @pl.when(me == 0)
    def _():
        clear(0)

    @pl.when(me == slabs - 1)
    def _():
        clear(HALO + cx)

    lead = shots // 2
    forward(0)

    for delta in range(1, slabs):
        rec_arrival(delta).wait_recv()
    for g in range(1, lead):
        forward(g)
    for p in range(slabs // 2):
        held_v[:, p * LANES : (p + 1) * LANES] = got_v[2 * p] + got_v[2 * p + 1]
    width = slabs // 2 * LANES

    def place_sources(step):
        where_lane = held_v[steps + 1 : steps + 2].astype(jnp.int32)
        hits = lax.broadcasted_iota(jnp.int32, (nz, width), 0) == where_lane
        rest = jnp.where(hits, held_v[step : step + 1], 0.0)
        for p in range(3):
            piece = rest.astype(jnp.bfloat16)
            rest = rest - piece.astype(jnp.float32)
            piece_v[p] = piece

    def add_sources(i):
        where_row = held_v[steps : steps + 1].astype(jnp.int32) - first_row(i)
        within = lax.broadcasted_iota(jnp.int32, (rows, width), 0)
        for x in range(cx):
            picks = jnp.where(within + x * ny == where_row, 1.0, 0.0).astype(jnp.bfloat16)
            total = None
            for p in range(3):
                term = lax.dot_general(
                    picks, piece_v[p], (((1,), (1,)), ((), ())), preferred_element_type=jnp.float32
                )
                total = term if total is None else total + term
            src_v[x] = total

    for copy in (load_now, load_old, load_cour, load_fwd):
        copy.wait()

    def img_copy(i):
        return pltpu.make_async_remote_copy(
            src_ref=img_send.at[i], dst_ref=img_recv.at[i],
            send_sem=img_ssem.at[i], recv_sem=img_rsem.at[i],
            device_id=(lax.rem(shot + 1 + i, shots), me), device_id_type=MESH,
        )

    def out_copy(which, i):
        at = first_row(i)
        if which == 0:
            return pltpu.make_async_copy(
                last_v.at[:, pl.ds(at, rows)], last_hbm.at[0, :, pl.ds(at, rows)], out_sem.at[0, i]
            )
        return pltpu.make_async_copy(
            ext.at[steps - 1, pl.ds(HALO, cx), pl.ds(at + PAD, rows)],
            prior_hbm.at[0, :, pl.ds(at, rows)], out_sem.at[1, i],
        )

    z_at = lax.broadcasted_iota(jnp.int32, (block_rows, nz), 1)

    def update(step, i):
        start = first_row(i)

        def block(b):
            at = pl.multiple_of(start + b * block_rows, block_rows)
            here = pl.ds(at, block_rows)
            padded = pl.ds(at + PAD, block_rows)
            held = pl.ds(pl.multiple_of(b * block_rows, block_rows), block_rows)
            layers = [ext[step, layer, padded, :] for layer in range(cx + 2 * HALO)]
            fields, images = [], []
            for x in range(cx):
                center = layers[HALO + x]
                summed = (3.0 * STENCIL_WEIGHTS[0]) * center
                for k in range(1, 5):
                    along = layers[HALO + x + k] + layers[HALO + x - k]
                    beside = ext[step, HALO + x, pl.ds(at + PAD + k, block_rows), :]
                    beside += ext[step, HALO + x, pl.ds(at + PAD - k, block_rows), :]
                    deep = jnp.where(z_at < nz - k, pltpu.roll(center, nz - k, 1), 0.0)
                    deep += jnp.where(z_at >= k, pltpu.roll(center, k, 1), 0.0)
                    summed += STENCIL_WEIGHTS[k] * (along + beside + deep)
                if step == 0:
                    before = old_v[x, here, :]
                else:
                    before = ext[step - 1, HALO + x, padded, :]
                source = src_v[x, held, :]
                fresh = 2.0 * center - before + cour_v[x, here, :] * (summed + source)
                image = fwd_v[step, x, here, :].astype(jnp.float32) * fresh
                if step > 0:
                    image += img_send[i, x, held, :]
                fields.append(fresh)
                images.append(image)
            for x in range(cx):
                if step < steps - 1:
                    ext[step + 1, HALO + x, padded, :] = fields[x]
                else:
                    last_v[x, here, :] = fields[x]
                img_send[i, x, held, :] = images[x]

        loop(rows // block_rows, block)

    for step in range(steps):
        place_sources(step)

        def chunk(i, step=step):
            ahead = step * shots + i + lead

            @pl.when(ahead < steps * shots)
            def _():
                forward(ahead)

            add_sources(i)
            wait_halo(step, i)
            update(step, i)
            if step < steps - 1:
                send_halo(step + 1, i)
            if step == steps - 2:
                out_copy(1, i).start()
            if step == steps - 1:
                out_copy(0, i).start()

                @pl.when(i < shots - 1)
                def _():
                    img_copy(i).start()

        loop(shots, chunk)

    for i in range(shots - 1):
        img_copy(i).wait_recv()
    for x in range(cx):
        total = img_send[shots - 1, x]
        for i in range(shots - 1):
            total += img_recv[i, x]
        image_ref[x] = total
    image_out = pltpu.make_async_copy(image_ref, image_hbm, load_sem.at[7])
    image_out.start()

    for step in range(steps):
        loop(shots, lambda i, step=step: wait_sent(step, i))
    for delta in range(1, slabs):
        rec_copy(delta).wait_send()
    for i in range(shots - 1):
        img_copy(i).wait_send()
    loop(steps * shots, forwarded)
    image_out.wait()
    loop(shots, lambda i: (out_copy(0, i).wait(), out_copy(1, i).wait()))


def store(count, *refs):
    loads, stores = [], []
    for at in range(count):
        source, target, held, sems = (refs[at + count * kind] for kind in range(4))
        for part in range(held.shape[0]):
            loads.append(pltpu.make_async_copy(source.at[part], held.at[part], sems.at[0, part]))
            stores.append(pltpu.make_async_copy(held.at[part], target.at[part], sems.at[1, part]))
    for load in loads:
        load.start()
    for load, write in zip(loads, stores):
        load.wait()
        write.start()
    for write in stores:
        write.wait()


def solution(mesh):
    slabs, shots = mesh.shape["space"], mesh.shape["shot"]

    def local(courant, now, old, receiver_slab, receiver_cell, residuals, forward):
        cx, ny, nz = courant.shape
        steps = residuals.shape[1]
        rows = ny // shots
        block_rows = min(32, rows)
        anywhere = pl.BlockSpec(memory_space=pl.ANY)
        f32 = jnp.float32
        dma = pltpu.SemaphoreType.DMA
        hbm = pl.BlockSpec(memory_space=pltpu.HBM)
        parts = pl.pallas_call(
            functools.partial(kernel, slabs, shots, steps, (cx, ny, nz), block_rows),
            out_shape=(
                jax.ShapeDtypeStruct((1, cx, ny, nz), f32),
                jax.ShapeDtypeStruct((1, cx, ny, nz), f32),
                jax.ShapeDtypeStruct((cx, rows, nz), f32),
            ),
            in_specs=[hbm] * 7,
            out_specs=(anywhere,) * 3,
            scratch_shapes=[
                pltpu.VMEM(receiver_cell.shape, jnp.int32),
                pltpu.VMEM(receiver_cell.shape, jnp.int32),
                pltpu.VMEM((steps, 1, receiver_cell.shape[1]), f32),
                pltpu.VMEM((steps, cx + 2 * HALO, ny + 2 * PAD, nz), f32),
                pltpu.VMEM((cx, ny, nz), f32),
                pltpu.VMEM((cx, ny, nz), f32),
                pltpu.VMEM(forward.shape[1:], forward.dtype),
                pltpu.VMEM((cx, ny, nz), f32),
                pltpu.VMEM((cx, rows, nz), f32),
                pltpu.VMEM((PACK, slabs // 2 * LANES), f32),
                pltpu.VMEM((3, nz, slabs // 2 * LANES), jnp.bfloat16),
                pltpu.VMEM((PACK, receiver_cell.shape[1]), f32),
                pltpu.VMEM((slabs, PACK, LANES), f32),
                pltpu.VMEM((slabs, PACK, LANES), f32),
                pltpu.VMEM((shots, cx, rows, nz), f32),
                pltpu.VMEM((shots, cx, rows, nz), f32),
                pltpu.VMEM((cx, rows, nz), f32),
                pltpu.VMEM((steps * shots, cx // 2, rows, nz), f32),
                dma((8,)),
                dma((2, shots)),
                dma((steps, 2, shots)),
                dma((steps, 2, shots)),
                dma((slabs,)),
                dma((slabs,)),
                dma((shots,)),
                dma((shots,)),
                dma((steps, 2, shots)),
                dma((steps, 2, shots)),
                dma((steps * shots,)),
                dma((steps * shots,)),
            ],
            compiler_params=pltpu.CompilerParams(
                collective_id=0, has_side_effects=True, vmem_limit_bytes=VMEM_BYTES
            ),
        )(
            receiver_slab.reshape(receiver_cell.shape), receiver_cell,
            jnp.transpose(residuals, (1, 0, 2)), now, old, courant, forward,
        )
        last, prior = (part.reshape(cx, ny, nz) for part in parts[:2])
        last, prior, image = pl.pallas_call(
            functools.partial(store, 3),
            out_shape=tuple(jax.ShapeDtypeStruct(part.shape, f32) for part in (last, prior, parts[2])),
            in_specs=[anywhere] * 3,
            out_specs=(hbm,) * 3,
            scratch_shapes=[pltpu.VMEM(part.shape, f32) for part in (last, prior, parts[2])] + [dma((2, cx))] * 3,
            compiler_params=pltpu.CompilerParams(vmem_limit_bytes=VMEM_BYTES),
        )(last, prior, parts[2])
        return last[None], prior[None], image

    in_specs = (
        P("space", None, None),
        P("shot", "space", None, None),
        P("shot", "space", None, None),
        P("shot", "space", None),
        P("shot", "space"),
        P("shot", None, "space"),
        P("shot", None, "space", None, None),
    )
    out_specs = (
        P("shot", "space", None, None),
        P("shot", "space", None, None),
        P("space", "shot", None),
    )
    return jax.shard_map(local, mesh=mesh, in_specs=in_specs, out_specs=out_specs, check_vma=False)
```

```python
import functools

import jax
import jax.numpy as jnp
from jax import lax
from jax.experimental import pallas as pl
from jax.experimental.pallas import tpu as pltpu
from jax.sharding import PartitionSpec as P

CAP = 48
HALO = 4
PAD = 8
LANES = 128
VMEM_BYTES = 62 * 1024 * 1024
PACK = 8
MESH = pl.DeviceIdType.MESH
STENCIL_WEIGHTS = (-205.0 / 72.0, 8.0 / 5.0, -1.0 / 5.0, 8.0 / 315.0, -1.0 / 560.0)


def kernel(
    slabs, shots, steps, extent, block_rows,
    slab_hbm, cell_hbm, res_hbm, now_hbm, old_hbm, cour_hbm, fwd_hbm,
    last_hbm, prior_hbm, image_hbm,
    slab_ref, cell_ref, res_ref, ext, old_v, cour_v, fwd_v, last_v, src_v, held_v, piece_v, data_v, pack_v, got_v, img_send, img_recv, image_ref, relay_v,
    load_sem, out_sem, halo_send, halo_recv, rec_send, rec_recv, img_ssem, img_rsem,
    diag_send, diag_recv, relay_send, relay_recv,
):
    cx, ny, nz = extent
    rows = ny // shots
    me = lax.axis_index("space")
    shot = lax.axis_index("shot")

    load_now = pltpu.make_async_copy(
        now_hbm.at[0], ext.at[0, pl.ds(HALO, cx), pl.ds(PAD, ny)], load_sem.at[0]
    )
    load_old = pltpu.make_async_copy(old_hbm.at[0], old_v, load_sem.at[1])
    load_cour = pltpu.make_async_copy(cour_hbm, cour_v, load_sem.at[2])
    load_fwd = pltpu.make_async_copy(fwd_hbm.at[0], fwd_v, load_sem.at[3])
    small_loads = [
        pltpu.make_async_copy(source, target, load_sem.at[4 + at])
        for at, (source, target) in enumerate(
            ((slab_hbm, slab_ref), (cell_hbm, cell_ref), (res_hbm, res_ref))
        )
    ]
    for copy in (*small_loads, load_now, load_old, load_cour, load_fwd):
        copy.start()

    barrier = pltpu.get_barrier_semaphore()
    for delta in range(1, slabs):
        pl.semaphore_signal(
            barrier, inc=1, device_id=(shot, lax.rem(me + delta, slabs)), device_id_type=MESH
        )
    for delta in range(1, shots):
        pl.semaphore_signal(
            barrier, inc=1, device_id=(lax.rem(shot + delta, shots), me), device_id_type=MESH
        )
    pl.semaphore_wait(barrier, slabs - 1 + shots - 1)

    def first_row(i):
        return pl.multiple_of(lax.rem(shot + 1 + i, shots) * rows, rows)

    def halo_copy(step, i, side):
        at = first_row(i)
        if step == 0:
            source = now_hbm.at[0, :, pl.ds(at, rows)]
        else:
            source = ext.at[step, pl.ds(HALO, cx), pl.ds(at + PAD, rows)]
        low_at = HALO + cx if side == 0 else 0
        return pltpu.make_async_remote_copy(
            src_ref=source,
            dst_ref=ext.at[step, pl.ds(low_at, HALO), pl.ds(at + PAD, rows)],
            send_sem=halo_send.at[step, side, i],
            recv_sem=halo_recv.at[step, side, i],
            device_id=(shot, me - 1 if side == 0 else me + 1),
            device_id_type=MESH,
        )

    quad = slabs % 4 == 0 and cx % 2 == 0
    half = cx // 2
    turn = lax.rem(me, 4)
    has_low, has_high = me > 0, me < slabs - 1
    if quad:
        diag_low, diag_high = has_low & (turn == 0), has_high & (turn == 3)
        near_low, near_high = has_low & (turn != 0), has_high & (turn != 3)
        relay_lower, relay_upper = (turn == 0) & (me + 4 < slabs), (turn == 3) & (me >= 7)
    else:
        near_low, near_high = has_low, has_high

    def diag_copy(step, i, up, h):
        at = first_row(i)
        if step == 0:
            source = now_hbm.at[0, pl.ds(h * half, half), pl.ds(at, rows)]
        else:
            source = ext.at[step, pl.ds(HALO + h * half, half), pl.ds(at + PAD, rows)]
        if h == 0:
            target = ext.at[step, pl.ds(0 if up else HALO + cx, half), pl.ds(at + PAD, rows)]
            arrived, to = diag_recv.at[step, 0, i], me + 1 if up else me - 1
        else:
            target = relay_v.at[step * shots + i]
            arrived, to = relay_recv.at[step * shots + i], me + 4 if up else me - 4
        return pltpu.make_async_remote_copy(
            src_ref=source, dst_ref=target, send_sem=diag_send.at[step, h, i], recv_sem=arrived,
            device_id=(shot, to), device_id_type=MESH,
        )

    def relay_copy(g, up):
        step, i = lax.div(g, shots), lax.rem(g, shots)
        low_at = (0 if up else HALO + cx) + half
        return pltpu.make_async_remote_copy(
            src_ref=relay_v.at[g],
            dst_ref=ext.at[step, pl.ds(low_at, half), pl.ds(first_row(i) + PAD, rows)],
            send_sem=relay_send.at[g],
            recv_sem=diag_recv.at[step, 1, i],
            device_id=(shot, me - 3 if up else me + 3),
            device_id_type=MESH,
        )

    def forward(g):
        if quad:
            for up, here in ((False, relay_lower), (True, relay_upper)):

                @pl.when(here)
                def _(up=up):
                    slot = relay_v.at[g]
                    pltpu.make_async_remote_copy(
                        src_ref=slot, dst_ref=slot, send_sem=relay_send.at[g], recv_sem=relay_recv.at[g],
                        device_id=(shot, me), device_id_type=MESH,
                    ).wait_recv()
                    relay_copy(g, up).start()

    def forwarded(g):
        if quad:
            for up, here in ((False, relay_lower), (True, relay_upper)):

                @pl.when(here)
                def _(up=up):
                    relay_copy(g, up).wait_send()

    def send_halo(step, i):
        @pl.when(near_low)
        def _():
            halo_copy(step, i, 0).start()

        @pl.when(near_high)
        def _():
            halo_copy(step, i, 1).start()

        if quad:
            for up, here in ((False, diag_low), (True, diag_high)):

                @pl.when(here)
                def _(up=up):
                    for h in (1, 0):
                        diag_copy(step, i, up, h).start()

    def wait_halo(step, i):
        @pl.when(near_high)
        def _():
            halo_copy(step, i, 0).wait_recv()

        @pl.when(near_low)
        def _():
            halo_copy(step, i, 1).wait_recv()

        if quad:
            for up, here in ((True, diag_low), (False, diag_high)):

                @pl.when(here)
                def _(up=up):
                    for h in range(2):
                        low_at = (0 if up else HALO + cx) + h * half
                        slot = ext.at[step, pl.ds(low_at, half), pl.ds(first_row(i) + PAD, rows)]
                        pltpu.make_async_remote_copy(
                            src_ref=slot, dst_ref=slot,
                            send_sem=diag_send.at[step, h, i],
                            recv_sem=diag_recv.at[step, h, i],
                            device_id=(shot, me), device_id_type=MESH,
                        ).wait_recv()

    def wait_sent(step, i):
        if quad:
            for up, here in ((False, diag_low), (True, diag_high)):

                @pl.when(here)
                def _(up=up):
                    for h in range(2):
                        diag_copy(step, i, up, h).wait_send()

        @pl.when(near_low)
        def _():
            halo_copy(step, i, 0).wait_send()

        @pl.when(near_high)
        def _():
            halo_copy(step, i, 1).wait_send()

    def loop(count, body):
        lax.fori_loop(0, count, lambda i, c: (body(i), c)[1], 0)

    send_halo(0, 0)

    for copy in small_loads:
        copy.wait()
    count = slab_ref.shape[1]
    row = slab_ref[...]
    cells = cell_ref[...]
    first = lax.broadcasted_iota(jnp.int32, (count, count), 0)
    second = lax.broadcasted_iota(jnp.int32, (count, count), 1)
    column = jnp.sum(jnp.where(first == second, row, 0), axis=1, keepdims=True)
    earlier = jnp.where((column == row) & (first < second), 1, 0)
    rank = jnp.sum(earlier, axis=0, keepdims=True)
    lane = rank + lax.rem(me, 2) * CAP
    data_v[...] = jnp.zeros_like(data_v)
    for step in range(steps):
        data_v[step : step + 1] = res_ref[step]
    data_v[steps : steps + 1] = lax.div(cells, nz).astype(jnp.float32)
    data_v[steps + 1 : steps + 2] = lax.rem(cells, nz).astype(jnp.float32)
    slots = lax.broadcasted_iota(jnp.int32, (LANES, count), 0)
    left, pieces = data_v[...], []
    for _ in range(3):
        pieces.append(left.astype(jnp.bfloat16).astype(jnp.float32))
        left = left - pieces[-1]
    pieces = jnp.concatenate(pieces, axis=0).astype(jnp.bfloat16)

    def pack(d):
        onehot = jnp.where((slots == lane) & (row == d), 1.0, 0.0).astype(jnp.bfloat16)
        packed = lax.dot_general(
            pieces, onehot, (((1,), (1,)), ((), ())), preferred_element_type=jnp.float32
        )
        pack_v[d] = packed[:PACK] + packed[PACK : 2 * PACK] + packed[2 * PACK :]

    def rec_copy(delta):
        to = lax.rem(me + delta, slabs)
        return pltpu.make_async_remote_copy(
            src_ref=pack_v.at[to], dst_ref=got_v.at[me],
            send_sem=rec_send.at[to], recv_sem=rec_recv.at[me],
            device_id=(shot, to), device_id_type=MESH,
        )

    def rec_arrival(delta):
        source = lax.rem(me + delta, slabs)
        return pltpu.make_async_remote_copy(
            src_ref=pack_v.at[source], dst_ref=got_v.at[source],
            send_sem=rec_send.at[source], recv_sem=rec_recv.at[source],
            device_id=(shot, source), device_id_type=MESH,
        )

    loop(slabs, pack)
    for delta in range(1, slabs):
        rec_copy(delta).start()
    loop(shots - 1, lambda i: send_halo(0, i + 1))
    got_v[me] = pack_v[me]

    edge = jnp.zeros((cx, PAD, nz), jnp.float32)
    for step in range(steps):
        ext[step, HALO : HALO + cx, 0:PAD] = edge
        ext[step, HALO : HALO + cx, PAD + ny :] = edge

    def clear(low_at):
        for step in range(steps):
            for layer in range(HALO):
                ext[step, low_at + layer] = jnp.zeros((ny + 2 * PAD, nz), jnp.float32)

    @pl.when(me == 0)
    def _():
        clear(0)

    @pl.when(me == slabs - 1)
    def _():
        clear(HALO + cx)

    lead = shots // 2
    forward(0)

    for delta in range(1, slabs):
        rec_arrival(delta).wait_recv()
    for g in range(1, lead):
        forward(g)
    for p in range(slabs // 2):
        held_v[:, p * LANES : (p + 1) * LANES] = got_v[2 * p] + got_v[2 * p + 1]
    width = slabs // 2 * LANES

    def place_sources(step):
        where_lane = held_v[steps + 1 : steps + 2].astype(jnp.int32)
        hits = lax.broadcasted_iota(jnp.int32, (nz, width), 0) == where_lane
        rest = jnp.where(hits, held_v[step : step + 1], 0.0)
        for p in range(3):
            piece = rest.astype(jnp.bfloat16)
            rest = rest - piece.astype(jnp.float32)
            piece_v[p] = piece

    def add_sources(i):
        where_row = held_v[steps : steps + 1].astype(jnp.int32) - first_row(i)
        within = lax.broadcasted_iota(jnp.int32, (rows, width), 0)
        for x in range(cx):
            picks = jnp.where(within + x * ny == where_row, 1.0, 0.0).astype(jnp.bfloat16)
            total = None
            for p in range(3):
                term = lax.dot_general(
                    picks, piece_v[p], (((1,), (1,)), ((), ())), preferred_element_type=jnp.float32
                )
                total = term if total is None else total + term
            src_v[x] = total

    for copy in (load_now, load_old, load_cour, load_fwd):
        copy.wait()

    def img_copy(i):
        return pltpu.make_async_remote_copy(
            src_ref=img_send.at[i], dst_ref=img_recv.at[i],
            send_sem=img_ssem.at[i], recv_sem=img_rsem.at[i],
            device_id=(lax.rem(shot + 1 + i, shots), me), device_id_type=MESH,
        )

    def out_copy(which, i):
        at = first_row(i)
        if which == 0:
            return pltpu.make_async_copy(
                last_v.at[:, pl.ds(at, rows)], last_hbm.at[0, :, pl.ds(at, rows)], out_sem.at[0, i]
            )
        return pltpu.make_async_copy(
            ext.at[steps - 1, pl.ds(HALO, cx), pl.ds(at + PAD, rows)],
            prior_hbm.at[0, :, pl.ds(at, rows)], out_sem.at[1, i],
        )

    z_at = lax.broadcasted_iota(jnp.int32, (block_rows, nz), 1)

    def update(step, i):
        start = first_row(i)

        def block(b):
            at = pl.multiple_of(start + b * block_rows, block_rows)
            here = pl.ds(at, block_rows)
            padded = pl.ds(at + PAD, block_rows)
            held = pl.ds(pl.multiple_of(b * block_rows, block_rows), block_rows)
            layers = [ext[step, layer, padded, :] for layer in range(cx + 2 * HALO)]
            fields, images = [], []
            for x in range(cx):
                center = layers[HALO + x]
                summed = (3.0 * STENCIL_WEIGHTS[0]) * center
                for k in range(1, 5):
                    along = layers[HALO + x + k] + layers[HALO + x - k]
                    beside = ext[step, HALO + x, pl.ds(at + PAD + k, block_rows), :]
                    beside += ext[step, HALO + x, pl.ds(at + PAD - k, block_rows), :]
                    deep = jnp.where(z_at < nz - k, pltpu.roll(center, nz - k, 1), 0.0)
                    deep += jnp.where(z_at >= k, pltpu.roll(center, k, 1), 0.0)
                    summed += STENCIL_WEIGHTS[k] * (along + beside + deep)
                if step == 0:
                    before = old_v[x, here, :]
                else:
                    before = ext[step - 1, HALO + x, padded, :]
                source = src_v[x, held, :]
                fresh = 2.0 * center - before + cour_v[x, here, :] * (summed + source)
                image = fwd_v[step, x, here, :].astype(jnp.float32) * fresh
                if step > 0:
                    image += img_send[i, x, held, :]
                fields.append(fresh)
                images.append(image)
            for x in range(cx):
                if step < steps - 1:
                    ext[step + 1, HALO + x, padded, :] = fields[x]
                else:
                    last_v[x, here, :] = fields[x]
                img_send[i, x, held, :] = images[x]

        loop(rows // block_rows, block)

    for step in range(steps):
        place_sources(step)

        def chunk(i, step=step):
            add_sources(i)
            wait_halo(step, i)
            update(step, i)
            if step < steps - 1:
                send_halo(step + 1, i)
            if step == steps - 2:
                out_copy(1, i).start()
            if step == steps - 1:
                out_copy(0, i).start()

                @pl.when(i < shots - 1)
                def _():
                    img_copy(i).start()

            ahead = step * shots + i + 1

            @pl.when((ahead >= lead) & (ahead < steps * shots))
            def _():
                forward(ahead)

        loop(shots, chunk)

    for i in range(shots - 1):
        img_copy(i).wait_recv()
    for x in range(cx):
        total = img_send[shots - 1, x]
        for i in range(shots - 1):
            total += img_recv[i, x]
        image_ref[x] = total
    image_out = pltpu.make_async_copy(image_ref, image_hbm, load_sem.at[7])
    image_out.start()

    for step in range(steps):
        loop(shots, lambda i, step=step: wait_sent(step, i))
    for delta in range(1, slabs):
        rec_copy(delta).wait_send()
    for i in range(shots - 1):
        img_copy(i).wait_send()
    loop(steps * shots, forwarded)
    image_out.wait()
    loop(shots, lambda i: (out_copy(0, i).wait(), out_copy(1, i).wait()))


def store(count, *refs):
    loads, stores = [], []
    for at in range(count):
        source, target, held, sems = (refs[at + count * kind] for kind in range(4))
        for part in range(held.shape[0]):
            loads.append(pltpu.make_async_copy(source.at[part], held.at[part], sems.at[0, part]))
            stores.append(pltpu.make_async_copy(held.at[part], target.at[part], sems.at[1, part]))
    for load in loads:
        load.start()
    for load, write in zip(loads, stores):
        load.wait()
        write.start()
    for write in stores:
        write.wait()


def solution(mesh):
    slabs, shots = mesh.shape["space"], mesh.shape["shot"]

    def local(courant, now, old, receiver_slab, receiver_cell, residuals, forward):
        cx, ny, nz = courant.shape
        steps = residuals.shape[1]
        rows = ny // shots
        block_rows = min(32, rows)
        anywhere = pl.BlockSpec(memory_space=pl.ANY)
        f32 = jnp.float32
        dma = pltpu.SemaphoreType.DMA
        hbm = pl.BlockSpec(memory_space=pltpu.HBM)
        parts = pl.pallas_call(
            functools.partial(kernel, slabs, shots, steps, (cx, ny, nz), block_rows),
            out_shape=(
                jax.ShapeDtypeStruct((1, cx, ny, nz), f32),
                jax.ShapeDtypeStruct((1, cx, ny, nz), f32),
                jax.ShapeDtypeStruct((cx, rows, nz), f32),
            ),
            in_specs=[hbm] * 7,
            out_specs=(anywhere,) * 3,
            scratch_shapes=[
                pltpu.VMEM(receiver_cell.shape, jnp.int32),
                pltpu.VMEM(receiver_cell.shape, jnp.int32),
                pltpu.VMEM((steps, 1, receiver_cell.shape[1]), f32),
                pltpu.VMEM((steps, cx + 2 * HALO, ny + 2 * PAD, nz), f32),
                pltpu.VMEM((cx, ny, nz), f32),
                pltpu.VMEM((cx, ny, nz), f32),
                pltpu.VMEM(forward.shape[1:], forward.dtype),
                pltpu.VMEM((cx, ny, nz), f32),
                pltpu.VMEM((cx, rows, nz), f32),
                pltpu.VMEM((PACK, slabs // 2 * LANES), f32),
                pltpu.VMEM((3, nz, slabs // 2 * LANES), jnp.bfloat16),
                pltpu.VMEM((PACK, receiver_cell.shape[1]), f32),
                pltpu.VMEM((slabs, PACK, LANES), f32),
                pltpu.VMEM((slabs, PACK, LANES), f32),
                pltpu.VMEM((shots, cx, rows, nz), f32),
                pltpu.VMEM((shots, cx, rows, nz), f32),
                pltpu.VMEM((cx, rows, nz), f32),
                pltpu.VMEM((steps * shots, cx // 2, rows, nz), f32),
                dma((8,)),
                dma((2, shots)),
                dma((steps, 2, shots)),
                dma((steps, 2, shots)),
                dma((slabs,)),
                dma((slabs,)),
                dma((shots,)),
                dma((shots,)),
                dma((steps, 2, shots)),
                dma((steps, 2, shots)),
                dma((steps * shots,)),
                dma((steps * shots,)),
            ],
            compiler_params=pltpu.CompilerParams(
                collective_id=0, has_side_effects=True, vmem_limit_bytes=VMEM_BYTES
            ),
        )(
            receiver_slab.reshape(receiver_cell.shape), receiver_cell,
            jnp.transpose(residuals, (1, 0, 2)), now, old, courant, forward,
        )
        last, prior = (part.reshape(cx, ny, nz) for part in parts[:2])
        last, prior, image = pl.pallas_call(
            functools.partial(store, 3),
            out_shape=tuple(jax.ShapeDtypeStruct(part.shape, f32) for part in (last, prior, parts[2])),
            in_specs=[anywhere] * 3,
            out_specs=(hbm,) * 3,
            scratch_shapes=[pltpu.VMEM(part.shape, f32) for part in (last, prior, parts[2])] + [dma((2, cx))] * 3,
            compiler_params=pltpu.CompilerParams(vmem_limit_bytes=VMEM_BYTES),
        )(last, prior, parts[2])
        return last[None], prior[None], image

    in_specs = (
        P("space", None, None),
        P("shot", "space", None, None),
        P("shot", "space", None, None),
        P("shot", "space", None),
        P("shot", "space"),
        P("shot", None, "space"),
        P("shot", None, "space", None, None),
    )
    out_specs = (
        P("shot", "space", None, None),
        P("shot", "space", None, None),
        P("space", "shot", None),
    )
    return jax.shard_map(local, mesh=mesh, in_specs=in_specs, out_specs=out_specs, check_vma=False)
```

```python
import functools

import jax
import jax.numpy as jnp
from jax import lax
from jax.experimental import pallas as pl
from jax.experimental.pallas import tpu as pltpu
from jax.sharding import PartitionSpec as P

CAP = 48
HALO = 4
PAD = 8
LANES = 128
VMEM_BYTES = 62 * 1024 * 1024
PACK = 8
MESH = pl.DeviceIdType.MESH
STENCIL_WEIGHTS = (-205.0 / 72.0, 8.0 / 5.0, -1.0 / 5.0, 8.0 / 315.0, -1.0 / 560.0)


def kernel(
    slabs, shots, steps, extent, block_rows,
    slab_hbm, cell_hbm, res_hbm, now_hbm, old_hbm, cour_hbm, fwd_hbm,
    last_hbm, prior_hbm, image_hbm,
    slab_ref, cell_ref, res_ref, ext, old_v, cour_v, fwd_v, last_v, src_v, held_v, piece_v, data_v, pack_v, got_v, img_send, img_recv, pre_v, image_ref, relay_v,
    load_sem, out_sem, halo_send, halo_recv, rec_send, rec_recv, img_ssem, img_rsem,
    diag_send, diag_recv, relay_send, relay_recv, pre_rsem,
):
    cx, ny, nz = extent
    rows = ny // shots
    me = lax.axis_index("space")
    shot = lax.axis_index("shot")

    load_now = pltpu.make_async_copy(
        now_hbm.at[0], ext.at[0, pl.ds(HALO, cx), pl.ds(PAD, ny)], load_sem.at[0]
    )
    load_old = pltpu.make_async_copy(old_hbm.at[0], old_v, load_sem.at[1])
    load_cour = pltpu.make_async_copy(cour_hbm, cour_v, load_sem.at[2])
    load_fwd = pltpu.make_async_copy(fwd_hbm.at[0], fwd_v, load_sem.at[3])
    small_loads = [
        pltpu.make_async_copy(source, target, load_sem.at[4 + at])
        for at, (source, target) in enumerate(
            ((slab_hbm, slab_ref), (cell_hbm, cell_ref), (res_hbm, res_ref))
        )
    ]
    for copy in (*small_loads, load_now, load_old, load_cour, load_fwd):
        copy.start()

    barrier = pltpu.get_barrier_semaphore()
    for delta in range(1, slabs):
        pl.semaphore_signal(
            barrier, inc=1, device_id=(shot, lax.rem(me + delta, slabs)), device_id_type=MESH
        )
    for delta in range(1, shots):
        pl.semaphore_signal(
            barrier, inc=1, device_id=(lax.rem(shot + delta, shots), me), device_id_type=MESH
        )
    pl.semaphore_wait(barrier, slabs - 1 + shots - 1)

    def target_shot(i):
        if shots & (shots - 1):
            return lax.rem(shot + 1 + i, shots)
        flips, target, bit = shots - 1 - i, 0, 1
        while bit < shots:
            target += lax.rem(lax.div(shot, bit) + lax.div(flips, bit), 2) * bit
            bit *= 2
        return target

    line = shots == 4
    outer = (shot == 0) | (shot == shots - 1)
    inner = (shot != 0) & (shot != shots - 1)

    def first_row(i):
        return pl.multiple_of(target_shot(i) * rows, rows)

    def halo_copy(step, i, side):
        at = first_row(i)
        if step == 0:
            source = now_hbm.at[0, :, pl.ds(at, rows)]
        else:
            source = ext.at[step, pl.ds(HALO, cx), pl.ds(at + PAD, rows)]
        low_at = HALO + cx if side == 0 else 0
        return pltpu.make_async_remote_copy(
            src_ref=source,
            dst_ref=ext.at[step, pl.ds(low_at, HALO), pl.ds(at + PAD, rows)],
            send_sem=halo_send.at[step, side, i],
            recv_sem=halo_recv.at[step, side, i],
            device_id=(shot, me - 1 if side == 0 else me + 1),
            device_id_type=MESH,
        )

    quad = slabs % 4 == 0 and cx % 2 == 0
    half = cx // 2
    turn = lax.rem(me, 4)
    has_low, has_high = me > 0, me < slabs - 1
    if quad:
        diag_low, diag_high = has_low & (turn == 0), has_high & (turn == 3)
        near_low, near_high = has_low & (turn != 0), has_high & (turn != 3)
        relay_lower, relay_upper = (turn == 0) & (me + 4 < slabs), (turn == 3) & (me >= 7)
    else:
        near_low, near_high = has_low, has_high

    def diag_copy(step, i, up, h):
        at = first_row(i)
        if step == 0:
            source = now_hbm.at[0, pl.ds(h * half, half), pl.ds(at, rows)]
        else:
            source = ext.at[step, pl.ds(HALO + h * half, half), pl.ds(at + PAD, rows)]
        if h == 0:
            target = ext.at[step, pl.ds(0 if up else HALO + cx, half), pl.ds(at + PAD, rows)]
            arrived, to = diag_recv.at[step, 0, i], me + 1 if up else me - 1
        else:
            target = relay_v.at[step * shots + i]
            arrived, to = relay_recv.at[step * shots + i], me + 4 if up else me - 4
        return pltpu.make_async_remote_copy(
            src_ref=source, dst_ref=target, send_sem=diag_send.at[step, h, i], recv_sem=arrived,
            device_id=(shot, to), device_id_type=MESH,
        )

    def relay_copy(g, up):
        step, i = lax.div(g, shots), lax.rem(g, shots)
        low_at = (0 if up else HALO + cx) + half
        return pltpu.make_async_remote_copy(
            src_ref=relay_v.at[g],
            dst_ref=ext.at[step, pl.ds(low_at, half), pl.ds(first_row(i) + PAD, rows)],
            send_sem=relay_send.at[g],
            recv_sem=diag_recv.at[step, 1, i],
            device_id=(shot, me - 3 if up else me + 3),
            device_id_type=MESH,
        )

    def forward(g):
        if quad:
            for up, here in ((False, relay_lower), (True, relay_upper)):

                @pl.when(here)
                def _(up=up):
                    slot = relay_v.at[g]
                    pltpu.make_async_remote_copy(
                        src_ref=slot, dst_ref=slot, send_sem=relay_send.at[g], recv_sem=relay_recv.at[g],
                        device_id=(shot, me), device_id_type=MESH,
                    ).wait_recv()
                    relay_copy(g, up).start()

    def forwarded(g):
        if quad:
            for up, here in ((False, relay_lower), (True, relay_upper)):

                @pl.when(here)
                def _(up=up):
                    relay_copy(g, up).wait_send()

    def send_halo(step, i):
        @pl.when(near_low)
        def _():
            halo_copy(step, i, 0).start()

        @pl.when(near_high)
        def _():
            halo_copy(step, i, 1).start()

        if quad:
            for up, here in ((False, diag_low), (True, diag_high)):

                @pl.when(here)
                def _(up=up):
                    for h in (1, 0):
                        diag_copy(step, i, up, h).start()

    def wait_halo(step, i):
        @pl.when(near_high)
        def _():
            halo_copy(step, i, 0).wait_recv()

        @pl.when(near_low)
        def _():
            halo_copy(step, i, 1).wait_recv()

        if quad:
            for up, here in ((True, diag_low), (False, diag_high)):

                @pl.when(here)
                def _(up=up):
                    for h in range(2):
                        low_at = (0 if up else HALO + cx) + h * half
                        slot = ext.at[step, pl.ds(low_at, half), pl.ds(first_row(i) + PAD, rows)]
                        pltpu.make_async_remote_copy(
                            src_ref=slot, dst_ref=slot,
                            send_sem=diag_send.at[step, h, i],
                            recv_sem=diag_recv.at[step, h, i],
                            device_id=(shot, me), device_id_type=MESH,
                        ).wait_recv()

    def wait_sent(step, i):
        if quad:
            for up, here in ((False, diag_low), (True, diag_high)):

                @pl.when(here)
                def _(up=up):
                    for h in range(2):
                        diag_copy(step, i, up, h).wait_send()

        @pl.when(near_low)
        def _():
            halo_copy(step, i, 0).wait_send()

        @pl.when(near_high)
        def _():
            halo_copy(step, i, 1).wait_send()

    def loop(count, body):
        lax.fori_loop(0, count, lambda i, c: (body(i), c)[1], 0)

    send_halo(0, 0)

    for copy in small_loads:
        copy.wait()
    count = slab_ref.shape[1]
    row = slab_ref[...]
    cells = cell_ref[...]
    first = lax.broadcasted_iota(jnp.int32, (count, count), 0)
    second = lax.broadcasted_iota(jnp.int32, (count, count), 1)
    column = jnp.sum(jnp.where(first == second, row, 0), axis=1, keepdims=True)
    earlier = jnp.where((column == row) & (first < second), 1, 0)
    rank = jnp.sum(earlier, axis=0, keepdims=True)
    lane = rank + lax.rem(me, 2) * CAP
    data_v[...] = jnp.zeros_like(data_v)
    for step in range(steps):
        data_v[step : step + 1] = res_ref[step]
    data_v[steps : steps + 1] = lax.div(cells, nz).astype(jnp.float32)
    data_v[steps + 1 : steps + 2] = lax.rem(cells, nz).astype(jnp.float32)
    slots = lax.broadcasted_iota(jnp.int32, (LANES, count), 0)
    left, pieces = data_v[...], []
    for _ in range(3):
        pieces.append(left.astype(jnp.bfloat16).astype(jnp.float32))
        left = left - pieces[-1]
    pieces = jnp.concatenate(pieces, axis=0).astype(jnp.bfloat16)

    def pack(d):
        onehot = jnp.where((slots == lane) & (row == d), 1.0, 0.0).astype(jnp.bfloat16)
        packed = lax.dot_general(
            pieces, onehot, (((1,), (1,)), ((), ())), preferred_element_type=jnp.float32
        )
        pack_v[d] = packed[:PACK] + packed[PACK : 2 * PACK] + packed[2 * PACK :]

    def rec_copy(delta):
        to = lax.rem(me + delta, slabs)
        return pltpu.make_async_remote_copy(
            src_ref=pack_v.at[to], dst_ref=got_v.at[me],
            send_sem=rec_send.at[to], recv_sem=rec_recv.at[me],
            device_id=(shot, to), device_id_type=MESH,
        )

    def rec_arrival(delta):
        source = lax.rem(me + delta, slabs)
        return pltpu.make_async_remote_copy(
            src_ref=pack_v.at[source], dst_ref=got_v.at[source],
            send_sem=rec_send.at[source], recv_sem=rec_recv.at[source],
            device_id=(shot, source), device_id_type=MESH,
        )

    loop(slabs, pack)
    for delta in range(1, slabs):
        rec_copy(delta).start()
    loop(shots - 1, lambda i: send_halo(0, i + 1))
    got_v[me] = pack_v[me]

    edge = jnp.zeros((cx, PAD, nz), jnp.float32)
    for step in range(steps):
        ext[step, HALO : HALO + cx, 0:PAD] = edge
        ext[step, HALO : HALO + cx, PAD + ny :] = edge

    def clear(low_at):
        for step in range(steps):
            for layer in range(HALO):
                ext[step, low_at + layer] = jnp.zeros((ny + 2 * PAD, nz), jnp.float32)

    if line:

        @pl.when(outer)
        def _():
            for x in range(cx):
                img_recv[0, x] = jnp.zeros((rows, nz), jnp.float32)

    @pl.when(me == 0)
    def _():
        clear(0)

    @pl.when(me == slabs - 1)
    def _():
        clear(HALO + cx)

    lead = shots // 2
    forward(0)

    for delta in range(1, slabs):
        rec_arrival(delta).wait_recv()
    for g in range(1, lead):
        forward(g)
    for p in range(slabs // 2):
        held_v[:, p * LANES : (p + 1) * LANES] = got_v[2 * p] + got_v[2 * p + 1]
    width = slabs // 2 * LANES

    def place_sources(step):
        where_lane = held_v[steps + 1 : steps + 2].astype(jnp.int32)
        hits = lax.broadcasted_iota(jnp.int32, (nz, width), 0) == where_lane
        rest = jnp.where(hits, held_v[step : step + 1], 0.0)
        for p in range(3):
            piece = rest.astype(jnp.bfloat16)
            rest = rest - piece.astype(jnp.float32)
            piece_v[p] = piece

    def add_sources(i):
        where_row = held_v[steps : steps + 1].astype(jnp.int32) - first_row(i)
        within = lax.broadcasted_iota(jnp.int32, (rows, width), 0)
        for x in range(cx):
            picks = jnp.where(within + x * ny == where_row, 1.0, 0.0).astype(jnp.bfloat16)
            total = None
            for p in range(3):
                term = lax.dot_general(
                    picks, piece_v[p], (((1,), (1,)), ((), ())), preferred_element_type=jnp.float32
                )
                total = term if total is None else total + term
            src_v[x] = total

    for copy in (load_now, load_old, load_cour, load_fwd):
        copy.wait()

    def img_copy(i):
        return pltpu.make_async_remote_copy(
            src_ref=img_send.at[i], dst_ref=img_recv.at[i],
            send_sem=img_ssem.at[i], recv_sem=img_rsem.at[i],
            device_id=(target_shot(i), me), device_id_type=MESH,
        )

    def pre_copy():
        return pltpu.make_async_remote_copy(
            src_ref=img_send.at[0], dst_ref=pre_v, send_sem=img_ssem.at[0], recv_sem=pre_rsem.at[0],
            device_id=(shot + 1 - 2 * lax.rem(shot, 2), me), device_id_type=MESH,
        )

    def out_copy(which, i):
        at = first_row(i)
        if which == 0:
            return pltpu.make_async_copy(
                last_v.at[:, pl.ds(at, rows)], last_hbm.at[0, :, pl.ds(at, rows)], out_sem.at[0, i]
            )
        return pltpu.make_async_copy(
            ext.at[steps - 1, pl.ds(HALO, cx), pl.ds(at + PAD, rows)],
            prior_hbm.at[0, :, pl.ds(at, rows)], out_sem.at[1, i],
        )

    z_at = lax.broadcasted_iota(jnp.int32, (block_rows, nz), 1)

    def update(step, i):
        start = first_row(i)

        def block(b):
            at = pl.multiple_of(start + b * block_rows, block_rows)
            here = pl.ds(at, block_rows)
            padded = pl.ds(at + PAD, block_rows)
            held = pl.ds(pl.multiple_of(b * block_rows, block_rows), block_rows)
            layers = [ext[step, layer, padded, :] for layer in range(cx + 2 * HALO)]
            fields, images = [], []
            for x in range(cx):
                center = layers[HALO + x]
                summed = (3.0 * STENCIL_WEIGHTS[0]) * center
                for k in range(1, 5):
                    along = layers[HALO + x + k] + layers[HALO + x - k]
                    beside = ext[step, HALO + x, pl.ds(at + PAD + k, block_rows), :]
                    beside += ext[step, HALO + x, pl.ds(at + PAD - k, block_rows), :]
                    deep = jnp.where(z_at < nz - k, pltpu.roll(center, nz - k, 1), 0.0)
                    deep += jnp.where(z_at >= k, pltpu.roll(center, k, 1), 0.0)
                    summed += STENCIL_WEIGHTS[k] * (along + beside + deep)
                if step == 0:
                    before = old_v[x, here, :]
                else:
                    before = ext[step - 1, HALO + x, padded, :]
                source = src_v[x, held, :]
                fresh = 2.0 * center - before + cour_v[x, here, :] * (summed + source)
                image = fwd_v[step, x, here, :].astype(jnp.float32) * fresh
                if step > 0:
                    image += img_send[i, x, held, :]
                fields.append(fresh)
                images.append(image)
            for x in range(cx):
                if step < steps - 1:
                    ext[step + 1, HALO + x, padded, :] = fields[x]
                else:
                    last_v[x, here, :] = fields[x]
                img_send[i, x, held, :] = images[x]

        loop(rows // block_rows, block)

    for step in range(steps):
        place_sources(step)

        def chunk(i, step=step):
            add_sources(i)
            wait_halo(step, i)
            update(step, i)
            if step < steps - 1:
                send_halo(step + 1, i)
            if step == steps - 2:
                out_copy(1, i).start()
            if step == steps - 1:
                out_copy(0, i).start()

                if line:

                    @pl.when((outer & (i > 0) & (i < shots - 1)) | (inner & ((i == 0) | (i == 2))))
                    def _():
                        img_copy(i).start()

                    @pl.when(outer & (i == 0))
                    def _():
                        pre_copy().start()

                    @pl.when(inner & (i == 2))
                    def _():
                        pre_copy().wait_recv()
                        for x in range(cx):
                            img_send[1, x] += pre_v[x]
                        img_copy(1).start()

                else:

                    @pl.when(i < shots - 1)
                    def _():
                        img_copy(i).start()

            ahead = step * shots + i + 1

            @pl.when((ahead >= lead) & (ahead < steps * shots))
            def _():
                forward(ahead)

        loop(shots, chunk)

    if line:

        @pl.when(inner)
        def _():
            img_copy(0).wait_recv()

    for i in range(1 if line else 0, shots - 1):
        img_copy(i).wait_recv()
    for x in range(cx):
        total = img_send[shots - 1, x]
        for i in range(shots - 1):
            total += img_recv[i, x]
        image_ref[x] = total
    image_out = pltpu.make_async_copy(image_ref, image_hbm, load_sem.at[7])
    image_out.start()

    for step in range(steps):
        loop(shots, lambda i, step=step: wait_sent(step, i))
    for delta in range(1, slabs):
        rec_copy(delta).wait_send()
    if line:

        @pl.when(outer)
        def _():
            pre_copy().wait_send()

        @pl.when(inner)
        def _():
            img_copy(0).wait_send()

    for i in range(1 if line else 0, shots - 1):
        img_copy(i).wait_send()
    loop(steps * shots, forwarded)
    image_out.wait()
    loop(shots, lambda i: (out_copy(0, i).wait(), out_copy(1, i).wait()))


def store(count, *refs):
    loads, stores = [], []
    for at in range(count):
        source, target, held, sems = (refs[at + count * kind] for kind in range(4))
        for part in range(held.shape[0]):
            loads.append(pltpu.make_async_copy(source.at[part], held.at[part], sems.at[0, part]))
            stores.append(pltpu.make_async_copy(held.at[part], target.at[part], sems.at[1, part]))
    for load in loads:
        load.start()
    for load, write in zip(loads, stores):
        load.wait()
        write.start()
    for write in stores:
        write.wait()


def solution(mesh):
    slabs, shots = mesh.shape["space"], mesh.shape["shot"]

    def local(courant, now, old, receiver_slab, receiver_cell, residuals, forward):
        cx, ny, nz = courant.shape
        steps = residuals.shape[1]
        rows = ny // shots
        block_rows = min(32, rows)
        anywhere = pl.BlockSpec(memory_space=pl.ANY)
        f32 = jnp.float32
        dma = pltpu.SemaphoreType.DMA
        hbm = pl.BlockSpec(memory_space=pltpu.HBM)
        parts = pl.pallas_call(
            functools.partial(kernel, slabs, shots, steps, (cx, ny, nz), block_rows),
            out_shape=(
                jax.ShapeDtypeStruct((1, cx, ny, nz), f32),
                jax.ShapeDtypeStruct((1, cx, ny, nz), f32),
                jax.ShapeDtypeStruct((cx, rows, nz), f32),
            ),
            in_specs=[hbm] * 7,
            out_specs=(anywhere,) * 3,
            scratch_shapes=[
                pltpu.VMEM(receiver_cell.shape, jnp.int32),
                pltpu.VMEM(receiver_cell.shape, jnp.int32),
                pltpu.VMEM((steps, 1, receiver_cell.shape[1]), f32),
                pltpu.VMEM((steps, cx + 2 * HALO, ny + 2 * PAD, nz), f32),
                pltpu.VMEM((cx, ny, nz), f32),
                pltpu.VMEM((cx, ny, nz), f32),
                pltpu.VMEM(forward.shape[1:], forward.dtype),
                pltpu.VMEM((cx, ny, nz), f32),
                pltpu.VMEM((cx, rows, nz), f32),
                pltpu.VMEM((PACK, slabs // 2 * LANES), f32),
                pltpu.VMEM((3, nz, slabs // 2 * LANES), jnp.bfloat16),
                pltpu.VMEM((PACK, receiver_cell.shape[1]), f32),
                pltpu.VMEM((slabs, PACK, LANES), f32),
                pltpu.VMEM((slabs, PACK, LANES), f32),
                pltpu.VMEM((shots, cx, rows, nz), f32),
                pltpu.VMEM((shots, cx, rows, nz), f32),
                pltpu.VMEM((cx, rows, nz), f32),
                pltpu.VMEM((cx, rows, nz), f32),
                pltpu.VMEM((steps * shots, cx // 2, rows, nz), f32),
                dma((8,)),
                dma((2, shots)),
                dma((steps, 2, shots)),
                dma((steps, 2, shots)),
                dma((slabs,)),
                dma((slabs,)),
                dma((shots,)),
                dma((shots,)),
                dma((steps, 2, shots)),
                dma((steps, 2, shots)),
                dma((steps * shots,)),
                dma((steps * shots,)),
                dma((1,)),
            ],
            compiler_params=pltpu.CompilerParams(
                collective_id=0, has_side_effects=True, vmem_limit_bytes=VMEM_BYTES
            ),
        )(
            receiver_slab.reshape(receiver_cell.shape), receiver_cell,
            jnp.transpose(residuals, (1, 0, 2)), now, old, courant, forward,
        )
        last, prior = (part.reshape(cx, ny, nz) for part in parts[:2])
        last, prior, image = pl.pallas_call(
            functools.partial(store, 3),
            out_shape=tuple(jax.ShapeDtypeStruct(part.shape, f32) for part in (last, prior, parts[2])),
            in_specs=[anywhere] * 3,
            out_specs=(hbm,) * 3,
            scratch_shapes=[pltpu.VMEM(part.shape, f32) for part in (last, prior, parts[2])] + [dma((2, cx))] * 3,
            compiler_params=pltpu.CompilerParams(vmem_limit_bytes=VMEM_BYTES),
        )(last, prior, parts[2])
        return last[None], prior[None], image

    in_specs = (
        P("space", None, None),
        P("shot", "space", None, None),
        P("shot", "space", None, None),
        P("shot", "space", None),
        P("shot", "space"),
        P("shot", None, "space"),
        P("shot", None, "space", None, None),
    )
    out_specs = (
        P("shot", "space", None, None),
        P("shot", "space", None, None),
        P("space", "shot", None),
    )
    return jax.shard_map(local, mesh=mesh, in_specs=in_specs, out_specs=out_specs, check_vma=False)
```

```python
import functools

import jax
import jax.numpy as jnp
from jax import lax
from jax.experimental import pallas as pl
from jax.experimental.pallas import tpu as pltpu
from jax.sharding import PartitionSpec as P

CAP = 48
HALO = 4
PAD = 8
LANES = 128
VMEM_BYTES = 62 * 1024 * 1024
PACK = 8
MESH = pl.DeviceIdType.MESH
STENCIL_WEIGHTS = (-205.0 / 72.0, 8.0 / 5.0, -1.0 / 5.0, 8.0 / 315.0, -1.0 / 560.0)


def kernel(
    slabs, shots, steps, extent, block_rows,
    slab_hbm, cell_hbm, res_hbm, now_hbm, old_hbm, cour_hbm, fwd_hbm,
    last_hbm, prior_hbm, image_hbm,
    slab_ref, cell_ref, res_ref, ext, old_v, cour_v, fwd_v, last_v, src_v, held_v, piece_v, data_v, pack_v, got_v, img_send, img_recv, pre_v, image_ref, relay_v,
    load_sem, out_sem, halo_send, halo_recv, rec_send, rec_recv, img_ssem, img_rsem,
    diag_send, diag_recv, relay_send, relay_recv, pre_rsem,
):
    cx, ny, nz = extent
    rows = ny // shots
    sub = 2 if rows % 64 == 0 else 1
    chunks, strip = shots * sub, rows // sub
    me = lax.axis_index("space")
    shot = lax.axis_index("shot")

    load_now = pltpu.make_async_copy(
        now_hbm.at[0], ext.at[0, pl.ds(HALO, cx), pl.ds(PAD, ny)], load_sem.at[0]
    )
    load_old = pltpu.make_async_copy(old_hbm.at[0], old_v, load_sem.at[1])
    load_cour = pltpu.make_async_copy(cour_hbm, cour_v, load_sem.at[2])
    load_fwd = pltpu.make_async_copy(fwd_hbm.at[0], fwd_v, load_sem.at[3])
    small_loads = [
        pltpu.make_async_copy(source, target, load_sem.at[4 + at])
        for at, (source, target) in enumerate(
            ((slab_hbm, slab_ref), (cell_hbm, cell_ref), (res_hbm, res_ref))
        )
    ]
    for copy in (*small_loads, load_now, load_old, load_cour, load_fwd):
        copy.start()

    barrier = pltpu.get_barrier_semaphore()
    for delta in range(1, slabs):
        pl.semaphore_signal(
            barrier, inc=1, device_id=(shot, lax.rem(me + delta, slabs)), device_id_type=MESH
        )
    for delta in range(1, shots):
        pl.semaphore_signal(
            barrier, inc=1, device_id=(lax.rem(shot + delta, shots), me), device_id_type=MESH
        )
    pl.semaphore_wait(barrier, slabs - 1 + shots - 1)

    def target_shot(i):
        if shots & (shots - 1):
            return lax.rem(shot + 1 + i, shots)
        flips, target, bit = shots - 1 - i, 0, 1
        while bit < shots:
            target += lax.rem(lax.div(shot, bit) + lax.div(flips, bit), 2) * bit
            bit *= 2
        return target

    line = shots == 4
    outer = (shot == 0) | (shot == shots - 1)
    inner = (shot != 0) & (shot != shots - 1)

    def first_row(i):
        return pl.multiple_of(target_shot(lax.div(i, sub)) * rows + lax.rem(i, sub) * strip, strip)

    def halo_copy(step, i, side):
        at = first_row(i)
        if step == 0:
            source = now_hbm.at[0, :, pl.ds(at, strip)]
        else:
            source = ext.at[step, pl.ds(HALO, cx), pl.ds(at + PAD, strip)]
        low_at = HALO + cx if side == 0 else 0
        return pltpu.make_async_remote_copy(
            src_ref=source,
            dst_ref=ext.at[step, pl.ds(low_at, HALO), pl.ds(at + PAD, strip)],
            send_sem=halo_send.at[step, side, i],
            recv_sem=halo_recv.at[step, side, i],
            device_id=(shot, me - 1 if side == 0 else me + 1),
            device_id_type=MESH,
        )

    quad = slabs % 4 == 0 and cx % 2 == 0
    half = cx // 2
    turn = lax.rem(me, 4)
    has_low, has_high = me > 0, me < slabs - 1
    if quad:
        diag_low, diag_high = has_low & (turn == 0), has_high & (turn == 3)
        near_low, near_high = has_low & (turn != 0), has_high & (turn != 3)
        relay_lower, relay_upper = (turn == 0) & (me + 4 < slabs), (turn == 3) & (me >= 7)
    else:
        near_low, near_high = has_low, has_high

    def diag_copy(step, i, up, h):
        at = first_row(i)
        if step == 0:
            source = now_hbm.at[0, pl.ds(h * half, half), pl.ds(at, strip)]
        else:
            source = ext.at[step, pl.ds(HALO + h * half, half), pl.ds(at + PAD, strip)]
        if h == 0:
            target = ext.at[step, pl.ds(0 if up else HALO + cx, half), pl.ds(at + PAD, strip)]
            arrived, to = diag_recv.at[step, 0, i], me + 1 if up else me - 1
        else:
            target = relay_v.at[step * chunks + i]
            arrived, to = relay_recv.at[step * chunks + i], me + 4 if up else me - 4
        return pltpu.make_async_remote_copy(
            src_ref=source, dst_ref=target, send_sem=diag_send.at[step, h, i], recv_sem=arrived,
            device_id=(shot, to), device_id_type=MESH,
        )

    def relay_copy(g, up):
        step, i = lax.div(g, chunks), lax.rem(g, chunks)
        low_at = (0 if up else HALO + cx) + half
        return pltpu.make_async_remote_copy(
            src_ref=relay_v.at[g],
            dst_ref=ext.at[step, pl.ds(low_at, half), pl.ds(first_row(i) + PAD, strip)],
            send_sem=relay_send.at[g],
            recv_sem=diag_recv.at[step, 1, i],
            device_id=(shot, me - 3 if up else me + 3),
            device_id_type=MESH,
        )

    def forward(g):
        if quad:
            for up, here in ((False, relay_lower), (True, relay_upper)):

                @pl.when(here)
                def _(up=up):
                    slot = relay_v.at[g]
                    pltpu.make_async_remote_copy(
                        src_ref=slot, dst_ref=slot, send_sem=relay_send.at[g], recv_sem=relay_recv.at[g],
                        device_id=(shot, me), device_id_type=MESH,
                    ).wait_recv()
                    relay_copy(g, up).start()

    def forwarded(g):
        if quad:
            for up, here in ((False, relay_lower), (True, relay_upper)):

                @pl.when(here)
                def _(up=up):
                    relay_copy(g, up).wait_send()

    def send_halo(step, i):
        @pl.when(near_low)
        def _():
            halo_copy(step, i, 0).start()

        @pl.when(near_high)
        def _():
            halo_copy(step, i, 1).start()

        if quad:
            for up, here in ((False, diag_low), (True, diag_high)):

                @pl.when(here)
                def _(up=up):
                    for h in (1, 0):
                        diag_copy(step, i, up, h).start()

    def wait_halo(step, i):
        @pl.when(near_high)
        def _():
            halo_copy(step, i, 0).wait_recv()

        @pl.when(near_low)
        def _():
            halo_copy(step, i, 1).wait_recv()

        if quad:
            for up, here in ((True, diag_low), (False, diag_high)):

                @pl.when(here)
                def _(up=up):
                    for h in range(2):
                        low_at = (0 if up else HALO + cx) + h * half
                        slot = ext.at[step, pl.ds(low_at, half), pl.ds(first_row(i) + PAD, strip)]
                        pltpu.make_async_remote_copy(
                            src_ref=slot, dst_ref=slot,
                            send_sem=diag_send.at[step, h, i],
                            recv_sem=diag_recv.at[step, h, i],
                            device_id=(shot, me), device_id_type=MESH,
                        ).wait_recv()

    def wait_sent(step, i):
        if quad:
            for up, here in ((False, diag_low), (True, diag_high)):

                @pl.when(here)
                def _(up=up):
                    for h in range(2):
                        diag_copy(step, i, up, h).wait_send()

        @pl.when(near_low)
        def _():
            halo_copy(step, i, 0).wait_send()

        @pl.when(near_high)
        def _():
            halo_copy(step, i, 1).wait_send()

    def loop(count, body):
        lax.fori_loop(0, count, lambda i, c: (body(i), c)[1], 0)

    send_halo(0, 0)

    for copy in small_loads:
        copy.wait()
    count = slab_ref.shape[1]
    row = slab_ref[...]
    cells = cell_ref[...]
    first = lax.broadcasted_iota(jnp.int32, (count, count), 0)
    second = lax.broadcasted_iota(jnp.int32, (count, count), 1)
    column = jnp.sum(jnp.where(first == second, row, 0), axis=1, keepdims=True)
    earlier = jnp.where((column == row) & (first < second), 1, 0)
    rank = jnp.sum(earlier, axis=0, keepdims=True)
    lane = rank + lax.rem(me, 2) * CAP
    data_v[...] = jnp.zeros_like(data_v)
    for step in range(steps):
        data_v[step : step + 1] = res_ref[step]
    data_v[steps : steps + 1] = lax.div(cells, nz).astype(jnp.float32)
    data_v[steps + 1 : steps + 2] = lax.rem(cells, nz).astype(jnp.float32)
    slots = lax.broadcasted_iota(jnp.int32, (LANES, count), 0)
    left, pieces = data_v[...], []
    for _ in range(3):
        pieces.append(left.astype(jnp.bfloat16).astype(jnp.float32))
        left = left - pieces[-1]
    pieces = jnp.concatenate(pieces, axis=0).astype(jnp.bfloat16)

    def pack(d):
        onehot = jnp.where((slots == lane) & (row == d), 1.0, 0.0).astype(jnp.bfloat16)
        packed = lax.dot_general(
            pieces, onehot, (((1,), (1,)), ((), ())), preferred_element_type=jnp.float32
        )
        pack_v[d] = packed[:PACK] + packed[PACK : 2 * PACK] + packed[2 * PACK :]

    def rec_copy(delta):
        to = lax.rem(me + delta, slabs)
        return pltpu.make_async_remote_copy(
            src_ref=pack_v.at[to], dst_ref=got_v.at[me],
            send_sem=rec_send.at[to], recv_sem=rec_recv.at[me],
            device_id=(shot, to), device_id_type=MESH,
        )

    def rec_arrival(delta):
        source = lax.rem(me + delta, slabs)
        return pltpu.make_async_remote_copy(
            src_ref=pack_v.at[source], dst_ref=got_v.at[source],
            send_sem=rec_send.at[source], recv_sem=rec_recv.at[source],
            device_id=(shot, source), device_id_type=MESH,
        )

    loop(slabs, pack)
    for delta in range(1, slabs):
        rec_copy(delta).start()
    loop(chunks - 1, lambda i: send_halo(0, i + 1))
    got_v[me] = pack_v[me]

    edge = jnp.zeros((cx, PAD, nz), jnp.float32)
    for step in range(steps):
        ext[step, HALO : HALO + cx, 0:PAD] = edge
        ext[step, HALO : HALO + cx, PAD + ny :] = edge

    def clear(low_at):
        for step in range(steps):
            for layer in range(HALO):
                ext[step, low_at + layer] = jnp.zeros((ny + 2 * PAD, nz), jnp.float32)

    if line:

        @pl.when(outer)
        def _():
            for x in range(cx):
                img_recv[0, x] = jnp.zeros((rows, nz), jnp.float32)

    @pl.when(me == 0)
    def _():
        clear(0)

    @pl.when(me == slabs - 1)
    def _():
        clear(HALO + cx)

    lead = chunks // 2
    forward(0)

    for delta in range(1, slabs):
        rec_arrival(delta).wait_recv()
    for g in range(1, lead):
        forward(g)
    for p in range(slabs // 2):
        held_v[:, p * LANES : (p + 1) * LANES] = got_v[2 * p] + got_v[2 * p + 1]
    width = slabs // 2 * LANES

    def place_sources(step):
        where_lane = held_v[steps + 1 : steps + 2].astype(jnp.int32)
        hits = lax.broadcasted_iota(jnp.int32, (nz, width), 0) == where_lane
        rest = jnp.where(hits, held_v[step : step + 1], 0.0)
        for p in range(3):
            piece = rest.astype(jnp.bfloat16)
            rest = rest - piece.astype(jnp.float32)
            piece_v[p] = piece

    def add_sources(i):
        where_row = held_v[steps : steps + 1].astype(jnp.int32) - first_row(i)
        within = lax.broadcasted_iota(jnp.int32, (strip, width), 0)
        for x in range(cx):
            picks = jnp.where(within + x * ny == where_row, 1.0, 0.0).astype(jnp.bfloat16)
            total = None
            for p in range(3):
                term = lax.dot_general(
                    picks, piece_v[p], (((1,), (1,)), ((), ())), preferred_element_type=jnp.float32
                )
                total = term if total is None else total + term
            src_v[x] = total

    for copy in (load_now, load_old, load_cour, load_fwd):
        copy.wait()

    def img_copy(i):
        return pltpu.make_async_remote_copy(
            src_ref=img_send.at[i], dst_ref=img_recv.at[i],
            send_sem=img_ssem.at[i], recv_sem=img_rsem.at[i],
            device_id=(target_shot(i), me), device_id_type=MESH,
        )

    def pre_copy():
        return pltpu.make_async_remote_copy(
            src_ref=img_send.at[0], dst_ref=pre_v, send_sem=img_ssem.at[0], recv_sem=pre_rsem.at[0],
            device_id=(shot + 1 - 2 * lax.rem(shot, 2), me), device_id_type=MESH,
        )

    def out_copy(which, i):
        at = first_row(i)
        if which == 0:
            return pltpu.make_async_copy(
                last_v.at[:, pl.ds(at, strip)], last_hbm.at[0, :, pl.ds(at, strip)], out_sem.at[0, i]
            )
        return pltpu.make_async_copy(
            ext.at[steps - 1, pl.ds(HALO, cx), pl.ds(at + PAD, strip)],
            prior_hbm.at[0, :, pl.ds(at, strip)], out_sem.at[1, i],
        )

    z_at = lax.broadcasted_iota(jnp.int32, (block_rows, nz), 1)

    def update(step, i):
        start = first_row(i)
        slot, base = lax.div(i, sub), lax.rem(i, sub) * strip

        def block(b):
            at = pl.multiple_of(start + b * block_rows, block_rows)
            here = pl.ds(at, block_rows)
            padded = pl.ds(at + PAD, block_rows)
            held = pl.ds(pl.multiple_of(base + b * block_rows, block_rows), block_rows)
            local = pl.ds(pl.multiple_of(b * block_rows, block_rows), block_rows)
            layers = [ext[step, layer, padded, :] for layer in range(cx + 2 * HALO)]
            fields, images = [], []
            for x in range(cx):
                center = layers[HALO + x]
                summed = (3.0 * STENCIL_WEIGHTS[0]) * center
                for k in range(1, 5):
                    along = layers[HALO + x + k] + layers[HALO + x - k]
                    beside = ext[step, HALO + x, pl.ds(at + PAD + k, block_rows), :]
                    beside += ext[step, HALO + x, pl.ds(at + PAD - k, block_rows), :]
                    deep = jnp.where(z_at < nz - k, pltpu.roll(center, nz - k, 1), 0.0)
                    deep += jnp.where(z_at >= k, pltpu.roll(center, k, 1), 0.0)
                    summed += STENCIL_WEIGHTS[k] * (along + beside + deep)
                if step == 0:
                    before = old_v[x, here, :]
                else:
                    before = ext[step - 1, HALO + x, padded, :]
                source = src_v[x, local, :]
                fresh = 2.0 * center - before + cour_v[x, here, :] * (summed + source)
                image = fwd_v[step, x, here, :].astype(jnp.float32) * fresh
                if step > 0:
                    image += img_send[slot, x, held, :]
                fields.append(fresh)
                images.append(image)
            for x in range(cx):
                if step < steps - 1:
                    ext[step + 1, HALO + x, padded, :] = fields[x]
                else:
                    last_v[x, here, :] = fields[x]
                img_send[slot, x, held, :] = images[x]

        loop(strip // block_rows, block)

    for step in range(steps):
        place_sources(step)

        def chunk(i, step=step):
            ahead = step * chunks + i + 1
            add_sources(i)
            wait_halo(step, i)
            update(step, i)
            if step < steps - 1:
                send_halo(step + 1, i)
            if step == steps - 2:
                out_copy(1, i).start()
            if step == steps - 1:
                out_copy(0, i).start()

                done = lax.rem(i, sub) == sub - 1
                i = lax.div(i, sub)
                if line:

                    @pl.when(done & ((outer & (i > 0) & (i < shots - 1)) | (inner & ((i == 0) | (i == 2)))))
                    def _():
                        img_copy(i).start()

                    @pl.when(done & outer & (i == 0))
                    def _():
                        pre_copy().start()

                    @pl.when(done & inner & (i == 2))
                    def _():
                        pre_copy().wait_recv()
                        for x in range(cx):
                            img_send[1, x] += pre_v[x]
                        img_copy(1).start()

                else:

                    @pl.when(done & (i < shots - 1))
                    def _():
                        img_copy(i).start()


            @pl.when((ahead >= lead) & (ahead < steps * chunks))
            def _():
                forward(ahead)

        loop(chunks, chunk)

    if line:

        @pl.when(inner)
        def _():
            img_copy(0).wait_recv()

    for i in range(1 if line else 0, shots - 1):
        img_copy(i).wait_recv()
    for x in range(cx):
        total = img_send[shots - 1, x]
        for i in range(shots - 1):
            total += img_recv[i, x]
        image_ref[x] = total
    image_out = pltpu.make_async_copy(image_ref, image_hbm, load_sem.at[7])
    image_out.start()

    for step in range(steps):
        loop(chunks, lambda i, step=step: wait_sent(step, i))
    for delta in range(1, slabs):
        rec_copy(delta).wait_send()
    if line:

        @pl.when(outer)
        def _():
            pre_copy().wait_send()

        @pl.when(inner)
        def _():
            img_copy(0).wait_send()

    for i in range(1 if line else 0, shots - 1):
        img_copy(i).wait_send()
    loop(steps * chunks, forwarded)
    image_out.wait()
    loop(chunks, lambda i: (out_copy(0, i).wait(), out_copy(1, i).wait()))


def store(count, *refs):
    loads, stores = [], []
    for at in range(count):
        source, target, held, sems = (refs[at + count * kind] for kind in range(4))
        for part in range(held.shape[0]):
            loads.append(pltpu.make_async_copy(source.at[part], held.at[part], sems.at[0, part]))
            stores.append(pltpu.make_async_copy(held.at[part], target.at[part], sems.at[1, part]))
    for load in loads:
        load.start()
    for load, write in zip(loads, stores):
        load.wait()
        write.start()
    for write in stores:
        write.wait()


def solution(mesh):
    slabs, shots = mesh.shape["space"], mesh.shape["shot"]

    def local(courant, now, old, receiver_slab, receiver_cell, residuals, forward):
        cx, ny, nz = courant.shape
        steps = residuals.shape[1]
        rows = ny // shots
        sub = 2 if rows % 64 == 0 else 1
        chunks, strip = shots * sub, rows // sub
        block_rows = min(32, strip)
        anywhere = pl.BlockSpec(memory_space=pl.ANY)
        f32 = jnp.float32
        dma = pltpu.SemaphoreType.DMA
        hbm = pl.BlockSpec(memory_space=pltpu.HBM)
        parts = pl.pallas_call(
            functools.partial(kernel, slabs, shots, steps, (cx, ny, nz), block_rows),
            out_shape=(
                jax.ShapeDtypeStruct((1, cx, ny, nz), f32),
                jax.ShapeDtypeStruct((1, cx, ny, nz), f32),
                jax.ShapeDtypeStruct((cx, rows, nz), f32),
            ),
            in_specs=[hbm] * 7,
            out_specs=(anywhere,) * 3,
            scratch_shapes=[
                pltpu.VMEM(receiver_cell.shape, jnp.int32),
                pltpu.VMEM(receiver_cell.shape, jnp.int32),
                pltpu.VMEM((steps, 1, receiver_cell.shape[1]), f32),
                pltpu.VMEM((steps, cx + 2 * HALO, ny + 2 * PAD, nz), f32),
                pltpu.VMEM((cx, ny, nz), f32),
                pltpu.VMEM((cx, ny, nz), f32),
                pltpu.VMEM(forward.shape[1:], forward.dtype),
                pltpu.VMEM((cx, ny, nz), f32),
                pltpu.VMEM((cx, strip, nz), f32),
                pltpu.VMEM((PACK, slabs // 2 * LANES), f32),
                pltpu.VMEM((3, nz, slabs // 2 * LANES), jnp.bfloat16),
                pltpu.VMEM((PACK, receiver_cell.shape[1]), f32),
                pltpu.VMEM((slabs, PACK, LANES), f32),
                pltpu.VMEM((slabs, PACK, LANES), f32),
                pltpu.VMEM((shots, cx, rows, nz), f32),
                pltpu.VMEM((shots, cx, rows, nz), f32),
                pltpu.VMEM((cx, rows, nz), f32),
                pltpu.VMEM((cx, rows, nz), f32),
                pltpu.VMEM((steps * chunks, cx // 2, strip, nz), f32),
                dma((8,)),
                dma((2, chunks)),
                dma((steps, 2, chunks)),
                dma((steps, 2, chunks)),
                dma((slabs,)),
                dma((slabs,)),
                dma((shots,)),
                dma((shots,)),
                dma((steps, 2, chunks)),
                dma((steps, 2, chunks)),
                dma((steps * chunks,)),
                dma((steps * chunks,)),
                dma((1,)),
            ],
            compiler_params=pltpu.CompilerParams(
                collective_id=0, has_side_effects=True, vmem_limit_bytes=VMEM_BYTES
            ),
        )(
            receiver_slab.reshape(receiver_cell.shape), receiver_cell,
            jnp.transpose(residuals, (1, 0, 2)), now, old, courant, forward,
        )
        last, prior = (part.reshape(cx, ny, nz) for part in parts[:2])
        last, prior, image = pl.pallas_call(
            functools.partial(store, 3),
            out_shape=tuple(jax.ShapeDtypeStruct(part.shape, f32) for part in (last, prior, parts[2])),
            in_specs=[anywhere] * 3,
            out_specs=(hbm,) * 3,
            scratch_shapes=[pltpu.VMEM(part.shape, f32) for part in (last, prior, parts[2])] + [dma((2, cx))] * 3,
            compiler_params=pltpu.CompilerParams(vmem_limit_bytes=VMEM_BYTES),
        )(last, prior, parts[2])
        return last[None], prior[None], image

    in_specs = (
        P("space", None, None),
        P("shot", "space", None, None),
        P("shot", "space", None, None),
        P("shot", "space", None),
        P("shot", "space"),
        P("shot", None, "space"),
        P("shot", None, "space", None, None),
    )
    out_specs = (
        P("shot", "space", None, None),
        P("shot", "space", None, None),
        P("space", "shot", None),
    )
    return jax.shard_map(local, mesh=mesh, in_specs=in_specs, out_specs=out_specs, check_vma=False)
```
